256 devices in a mesh: span: 16 (over z, x_hi), mp: 16 (over y, x_lo, core).
Axes of the slice: x: 4 (x_hi: 2, x_lo: 2; x = x_hi * 2 + x_lo), y: 4, z: 8, core: 2. Of those that a mesh axis runs over, the one named last changes fastest.
Arguments:
- queries: bfloat16 [12288, 6144], P('span', 'mp'), may hold values from -11 to 11
- keys: bfloat16 [12288, 6144], P('span', 'mp'), may hold values from -11 to 11
- values: bfloat16 [12288, 6144], P('span', 'mp'), may hold values from -6 to 6
- residual: bfloat16 [12288, 6144], P(('span', 'mp')), may hold values from -6 to 6
- out_weight: bfloat16 [6144, 6144], P('mp'), may hold values from -0.078125 to 0.078125
- gate_table: float32 [16, 6144], replicated, may hold values from 0.5 to 2
- noise_steps: int32 [16], replicated, may hold values from 0 to 15, each once
- windows: int32 [16, 2], replicated, may hold values 0 or 1
Outputs:
- mixed: bfloat16 [12288, 6144], P(('span', 'mp'))
The draws below stay inside these ranges and needn't reach their ends.
All inputs are finite; a program needn't handle non-finite values.
Results may differ from the reference program's by a relative error of at most 0.018.
Values may be sent and summed in bfloat16 or wider, within the bound.
No kernel may reach another device: no remote copies, remote signals or barrier semaphores. Data moves between devices by JAX's collectives and lax.ppermute only.
A program may use at most 64 MiB of HBM per device.

```python
import math
import jax
import jax.numpy as jnp
from jax import lax

D = 6144
HEADS = 48
HD = 128
CTOK = 768
LAGS = 2
TOKENS = 12288
N_SPAN = 16
N_MP = 16


def draw_queries(key, part):
    key = jax.random.fold_in(key, 11)
    drawn = jnp.clip(2.0 * jax.random.normal(key, (TOKENS, HEADS * HD), jnp.float32), -8.0, 8.0)
    return drawn.astype(jnp.bfloat16)


def draw_keys(key, part):
    key = jax.random.fold_in(key, 23)
    drawn = jnp.clip(jax.random.normal(key, (TOKENS, HEADS * HD), jnp.float32), -8.0, 8.0)
    return drawn.astype(jnp.bfloat16)


def plant(values, rng, smallest, high):
    place = [jax.random.randint(jax.random.fold_in(rng, axis), (), 0, length) for axis, length in enumerate(values.shape)]
    longest = values.shape.index(max(values.shape))
    neighbour = place[:longest] + [(place[longest] + 1) % values.shape[longest]] + place[longest + 1:]
    return values.at[tuple(place)].set(smallest).at[tuple(neighbour)].set(high)


def level_of(own_key, shape, cuts, low, top_value):
    def one(dim, shards_of):
        steps = jax.random.uniform(jax.random.fold_in(jax.random.fold_in(own_key, 6), dim), (shards_of,), jnp.float32, low / len(cuts), top_value / len(cuts))
        return jnp.repeat(jnp.exp(steps), shape[dim] // shards_of).reshape((-1,) + (1,) * (len(shape) - dim - 1))

    level = one(*cuts[0])
    for cut in cuts[1:]:
        level = level * one(*cut)
    return level


def centred(key, extent, scale, most, pieces=(), kind=jnp.bfloat16):
    level = level_of(key, extent, pieces, -0.22, 0.18) if pieces else 1.0
    values = jax.random.normal(key, extent, jnp.float32) * scale * level
    return jnp.minimum(jnp.maximum(values, -most), most).astype(kind)


def setup_inputs(seed: int = 0) -> dict:
    splits = jax.random.split(jax.random.key(seed), 9)
    queries = draw_queries(jax.random.fold_in(splits[8], 71), 0)
    keys = draw_keys(jax.random.fold_in(splits[8], 71), 0)
    values = centred(splits[2], (TOKENS, HEADS * HD), 1.0, 6.0, ((0, 16), (1, 16)))
    residual = centred(splits[3], (TOKENS, D), 1.0, 6.0, ((0, 256),))
    out_weight = centred(splits[4], (HEADS * HD, D), (HEADS * HD) ** -0.5, 0.078125, ((0, 16),))
    gate_table = jnp.clip(jnp.exp(jax.random.uniform(splits[5], (N_SPAN, D), jnp.float32, math.log(0.5), math.log(2.0))), 0.5, 2.0)
    noise_steps = jax.random.permutation(splits[6], N_SPAN).astype(jnp.int32)
    windows = plant((jax.random.randint(splits[7], (N_SPAN, LAGS), 0, 2) < 1).astype(jnp.int32), jax.random.fold_in(splits[7], 1), 0, 1)
    return dict(queries=queries, keys=keys, values=values, residual=residual, out_weight=out_weight, gate_table=gate_table, noise_steps=noise_steps, windows=windows)


def attend_head(query_rows, key_rows, value_rows, key_live):
    scores = jnp.dot(query_rows, key_rows.T, preferred_element_type=jnp.float32) * (HD ** -0.5)
    scores = jnp.where(key_live[None, :], scores, -1e30)
    row_peak = jnp.max(scores, axis=1, keepdims=True)
    exp_scores = jnp.exp(scores - row_peak)
    weights_bf = (exp_scores / jnp.sum(exp_scores, axis=1, keepdims=True)).astype(jnp.bfloat16)
    return jnp.dot(weights_bf, value_rows, preferred_element_type=jnp.float32).astype(jnp.bfloat16)


def reference(queries, keys, values, residual, out_weight, gate_table, noise_steps, windows):
    span_ids = jnp.arange(N_SPAN, dtype=jnp.int32)
    clean_root = jnp.sum(span_ids * (noise_steps == 0).astype(jnp.int32))
    full_width = HEADS * HD
    head_share = full_width // N_MP

    def rows_of(array, span):
        return lax.dynamic_slice_in_dim(array, (span * CTOK).astype(jnp.int32), CTOK, 0)

    def one_span(span):
        source_ids = [span, clean_root] + [(span - lag_index - 1) % N_SPAN for lag_index in range(LAGS)]
        live_flags = [span >= 0, span != clean_root] + [windows[span, lag_index] == 1 for lag_index in range(LAGS)]
        all_keys = jnp.concatenate([rows_of(keys, source) for source in source_ids], 0)
        all_values = jnp.concatenate([rows_of(values, source) for source in source_ids], 0)
        key_live = jnp.concatenate([jnp.broadcast_to(flag, (CTOK,)) for flag in live_flags])
        query_heads = rows_of(queries, span).reshape(CTOK, HEADS, HD).transpose(1, 0, 2)
        key_heads = all_keys.reshape(-1, HEADS, HD).transpose(1, 0, 2)
        value_heads = all_values.reshape(-1, HEADS, HD).transpose(1, 0, 2)
        attended = lax.map(lambda triple: attend_head(triple[0], triple[1], triple[2], key_live),
                           (query_heads, key_heads, value_heads))
        attended = attended.transpose(1, 0, 2).reshape(CTOK, full_width)
        group_rows = attended.reshape(CTOK, N_MP, head_share).transpose(1, 0, 2)
        group_weights = out_weight.reshape(N_MP, head_share, D)

        def add_group(summed, operands):
            partial_value = jnp.dot(operands[0], operands[1], preferred_element_type=jnp.float32).astype(jnp.bfloat16)
            partial_value = lax.optimization_barrier(partial_value)
            return summed + partial_value.astype(jnp.float32), None

        summed, _ = lax.scan(add_group, jnp.zeros((CTOK, D), jnp.float32), (group_rows, group_weights))
        selector = (span_ids == noise_steps[span]).astype(jnp.float32)
        gate_row = jnp.dot(selector, gate_table, precision=lax.Precision.HIGHEST)
        return (rows_of(residual, span).astype(jnp.float32) + gate_row[None, :] * summed).astype(jnp.bfloat16)

    mixed = lax.map(one_span, span_ids)
    return mixed.reshape(TOKENS, D)
```

```python
import math

import jax
import jax.numpy as jnp
from jax import lax
from jax.experimental import pallas as pl
from jax.experimental.pallas import tpu as pltpu
from jax.sharding import Mesh, PartitionSpec as P

HD = 128
HEADS_HERE = 3
NZ, NXH, NY, NXL, NC = 8, 2, 4, 2, 2
X_FIRST = 2688
LOG2E = math.log2(math.e)
SWAP = [(0, 1), (1, 0)]


def shift(value, axis, count, steps):
    return lax.ppermute(value, axis, [(i, (i + steps) % count) for i in range(count)])


def attend_body(scalar_ref, q_ref, k0, v0, k1, v1, k2, v2, *rest):
    pieces, (out_ref, peak_ref, total_ref, k3, v3) = rest[:NZ], rest[NZ:]
    factor = HD ** (-0.5) * LOG2E
    share = q_ref.shape[1]
    rows = k0.shape[0]
    piece_rows = rows // NZ
    y, xl, core = scalar_ref[4], scalar_ref[5], scalar_ref[6]
    step = pl.program_id(0)
    blocks = ((k0, v0), (k1, v1), (k2, v2), (k3, v3))
    ones = jnp.ones((rows, HD), jnp.bfloat16)

    @pl.when(step == 0)
    def _():
        for number, piece in enumerate(pieces):
            k3[pl.ds(number * piece_rows, piece_rows)] = piece[0]
            v3[pl.ds(number * piece_rows, piece_rows)] = piece[1]

    places = []
    for xl_step in range(NXL):
        for y_step in range(NY):
            y_there = lax.rem(y + y_step, NY)
            xl_there = lax.rem(xl + xl_step, NXL)
            places.append((y_there * NXL + xl_there) * NC + lax.rem(core + step, NC))

    def queries_of(head):
        return jnp.concatenate([q_ref[place, :, head * HD : (head + 1) * HD] for place in places], axis=0)

    for number, (k_ref, v_ref) in enumerate(blocks):

        def one_block(number=number, k_ref=k_ref, v_ref=v_ref):
            for head in range(HEADS_HERE):
                cols = slice(head * HD, (head + 1) * HD)
                scores = lax.dot_general(
                    queries_of(head), k_ref[:, cols], (((1,), (1,)), ((), ())), preferred_element_type=jnp.float32
                )
                block_peak = jnp.max(scores, axis=1, keepdims=True)
                if number == 0:
                    peak = block_peak
                else:
                    old_peak = peak_ref[head]
                    peak = jnp.maximum(old_peak, block_peak)
                probs = jnp.exp2((scores - peak) * factor).astype(jnp.bfloat16)
                wide = jnp.concatenate([v_ref[:, cols], ones], axis=1)
                added = jnp.dot(probs, wide, preferred_element_type=jnp.float32)
                if number == 0:
                    total_ref[head] = added
                else:
                    total_ref[head] = total_ref[head] * jnp.exp2((old_peak - peak) * factor) + added
                peak_ref[head] = peak

        if number == 0:
            one_block()
        else:
            pl.when(scalar_ref[number] == 1)(one_block)
    for head in range(HEADS_HERE):
        total = total_ref[head]
        out_ref[:, head * HD : (head + 1) * HD] = (total[:, :HD] / total[:, HD:]).astype(jnp.bfloat16)


def attend(scalars, queries, blocks, pieces):
    rows, width = queries.shape
    share = rows // (NY * NXL * NC)
    tile = rows // NC
    whole = pl.BlockSpec((rows, width), lambda i, *_: (0, 0))
    return pl.pallas_call(
        attend_body,
        out_shape=jax.ShapeDtypeStruct((rows, width), jnp.bfloat16),
        grid_spec=pltpu.PrefetchScalarGridSpec(
            num_scalar_prefetch=1,
            grid=(NC,),
            in_specs=[pl.BlockSpec((NY * NXL * NC, share, width), lambda i, *_: (0, 0, 0))]
            + [whole] * len(blocks)
            + [pl.BlockSpec((2, rows // NZ, width), lambda i, *_: (0, 0, 0))] * len(pieces),
            out_specs=pl.BlockSpec((tile, width), lambda i, *_: (i, 0)),
            scratch_shapes=[
                pltpu.VMEM((HEADS_HERE, tile, 1), jnp.float32),
                pltpu.VMEM((HEADS_HERE, tile, 2 * HD), jnp.float32),
                pltpu.VMEM((rows, width), jnp.bfloat16),
                pltpu.VMEM((rows, width), jnp.bfloat16),
            ],
        ),
        compiler_params=pltpu.CompilerParams(vmem_limit_bytes=40 * 1024 * 1024),
        cost_estimate=pl.CostEstimate(
            flops=16 * rows * rows * width, bytes_accessed=20 * rows * width, transcendentals=12 * rows * rows
        ),
    )(scalars, queries.reshape(NY * NXL * NC, share, width), *blocks, *pieces)


def spread_clean(keys, values, root, z, xh):
    rows, width = keys.shape
    own = jnp.stack([keys.reshape(NZ, rows // NZ, width), values.reshape(NZ, rows // NZ, width)], axis=1)
    distance = lax.rem(z - root // NXH + NZ, NZ)
    at_root = distance == 0
    up, down = own[4], own[5]
    for number in range(4):
        up = shift(jnp.where(at_root, own[4 - number], up) if number else up, "z", NZ, 1)
        if number < 3:
            down = shift(jnp.where(at_root, own[5 + number], down) if number else down, "z", NZ, -1)
    piece = jnp.where(at_root, own[0], jnp.where(distance <= 4, up, down))
    piece = jnp.where(xh == lax.rem(root, NXH), piece, lax.ppermute(piece, "xh", SWAP))
    pieces = [piece]
    up = down = piece
    for number in range(4):
        up = shift(up, "z", NZ, 1)
        pieces.append(up)
        if number < 3:
            down = shift(down, "z", NZ, -1)
            pieces.append(down)
    return pieces


def add(*terms):
    total = terms[0].astype(jnp.float32)
    for term in terms[1:]:
        total = total + term.astype(jnp.float32)
    return total


def sum_over_y(terms):
    half = terms[0].shape[-1] // 2
    from_below = shift(terms[2][..., :half], "y", NY, 1)
    from_above = shift(terms[2][..., half:], "y", NY, -1)
    rise = jnp.concatenate([add(terms[1][..., :half], from_below).astype(jnp.bfloat16), terms[1][..., half:]], axis=-1)
    fall = jnp.concatenate([terms[3][..., :half], add(terms[3][..., half:], from_above).astype(jnp.bfloat16)], axis=-1)
    return [terms[0], shift(rise, "y", NY, 1), shift(fall, "y", NY, -1)]


def local(queries, keys, values, residual, out_weight, gate_table, noise_steps, windows):
    z, xh, y, xl, core = (lax.axis_index(name) for name in ("z", "xh", "y", "xl", "c"))
    my_span = z * NXH + xh
    span_ids = lax.iota(jnp.int32, NZ * NXH)
    clean_root = jnp.sum(span_ids * (noise_steps == 0).astype(jnp.int32))
    rows, width = queries.shape
    share = residual.shape[0]

    lag2_keys, lag2_values = shift(keys, "z", NZ, 1), shift(values, "z", NZ, 1)
    pieces = spread_clean(keys, values, clean_root, z, xh)
    lag1_keys = lax.ppermute(jnp.where(xh == 0, keys, lag2_keys), "xh", SWAP)
    lag1_values = lax.ppermute(jnp.where(xh == 0, values, lag2_values), "xh", SWAP)
    sibling_weight = lax.ppermute(out_weight, "c", SWAP)

    scalars = jnp.stack(
        [
            jnp.int32(1),
            windows[my_span, 1],
            windows[my_span, 0],
            (my_span != clean_root).astype(jnp.int32),
            y,
            xl,
            core,
        ]
    )
    blocks = [keys, values, lag2_keys, lag2_values, lag1_keys, lag1_values]
    attended = attend(scalars, queries, blocks, pieces)
    taken = lax.ppermute(attended[rows // 2 :], "c", SWAP)
    both = jnp.concatenate([attended[: rows // 2], taken], axis=1)
    weight = jnp.concatenate([out_weight, sibling_weight], axis=0)

    def project(low, high):
        terms = jnp.dot(both, weight[:, low:high], preferred_element_type=jnp.float32).astype(jnp.bfloat16)
        return terms.reshape(NXL, NY, share, high - low)

    x_first = project(0, X_FIRST)
    y_first = project(X_FIRST, out_weight.shape[1])

    x_got = lax.ppermute(x_first[1], "xl", SWAP)
    here = sum_over_y([y_first[:, number] for number in range(NY)])
    here_kept = [term[0] for term in here]
    here_sent = add(*[term[1] for term in here]).astype(jnp.bfloat16)
    here_got = lax.ppermute(here_sent, "xl", SWAP)
    x_sum = add(x_first[0], x_got).astype(jnp.bfloat16)
    left = add(*sum_over_y([x_sum[number] for number in range(NY)]))
    right = add(*here_kept, here_got)
    gate_row = lax.dynamic_slice_in_dim(gate_table, noise_steps[my_span], 1, 0)
    summed = jnp.concatenate([left, right], axis=1)
    return (residual.astype(jnp.float32) + gate_row * summed).astype(jnp.bfloat16)


def solution(mesh):
    fine = Mesh(mesh.devices.reshape(NZ, NXH, NY, NXL, NC), ("z", "xh", "y", "xl", "c"))
    span, mp = ("z", "xh"), ("y", "xl", "c")
    in_specs = (
        P(span, mp),
        P(span, mp),
        P(span, mp),
        P(span + mp, None),
        P(mp, None),
        P(),
        P(),
        P(),
    )
    out_specs = P(span + mp, None)
    return jax.shard_map(local, mesh=fine, in_specs=in_specs, out_specs=out_specs, check_vma=False)
```

```python
import functools
import math

import jax
import jax.numpy as jnp
from jax import lax
from jax.experimental import pallas as pl
from jax.experimental.pallas import tpu as pltpu
from jax.sharding import Mesh, PartitionSpec as P

HD = 128
HEADS_HERE = 3
NZ, NXH, NY, NXL, NC = 8, 2, 4, 2, 2
X_FIRST = 2688
COLUMN_TILE = 384
LOG2E = math.log2(math.e)
SWAP = [(0, 1), (1, 0)]


def shift(value, axis, count, steps):
    return lax.ppermute(value, axis, [(i, (i + steps) % count) for i in range(count)])


def attend_body(number_of_blocks, first, last, *refs):
    refs = list(refs)
    scalar_ref, q_ref = refs.pop(0), refs.pop(0)
    blocks = []
    for _ in range(number_of_blocks - (1 if last else 0)):
        blocks.append((refs.pop(0), refs.pop(0)))
    step = pl.program_id(0)
    if last:
        pieces = [refs.pop(0) for _ in range(NZ)]
        old_peak_ref, old_total_ref, out_ref, peak_ref, total_ref, k_clean, v_clean = refs
        piece_rows = pieces[0].shape[1]

        @pl.when(step == 0)
        def _():
            for number, piece in enumerate(pieces):
                k_clean[pl.ds(number * piece_rows, piece_rows)] = piece[0]
                v_clean[pl.ds(number * piece_rows, piece_rows)] = piece[1]

        blocks.append((k_clean, v_clean))
        peak_ref[...] = old_peak_ref[...]
        total_ref[...] = old_total_ref[...]
    else:
        peak_ref, total_ref = refs
    factor = HD ** (-0.5) * LOG2E
    ones = jnp.ones((blocks[0][0].shape[0], HD), jnp.bfloat16)
    y, xl, core = scalar_ref[4], scalar_ref[5], scalar_ref[6]
    places = []
    for xl_step in range(NXL):
        for y_step in range(NY):
            y_there = lax.rem(y + y_step, NY)
            xl_there = lax.rem(xl + xl_step, NXL)
            places.append((y_there * NXL + xl_there) * NC + lax.rem(core + step, NC))

    def queries_of(head):
        return jnp.concatenate([q_ref[place, :, head * HD : (head + 1) * HD] for place in places], axis=0)

    for number, (k_ref, v_ref) in enumerate(blocks):
        fresh = number == 0 and not last

        def one_block(fresh=fresh, k_ref=k_ref, v_ref=v_ref):
            for head in range(HEADS_HERE):
                cols = slice(head * HD, (head + 1) * HD)
                scores = lax.dot_general(
                    queries_of(head), k_ref[:, cols], (((1,), (1,)), ((), ())), preferred_element_type=jnp.float32
                )
                peak = jnp.max(scores, axis=1, keepdims=True)
                if not fresh:
                    old_peak = peak_ref[head]
                    peak = jnp.maximum(old_peak, peak)
                    scaled = total_ref[head] * jnp.exp2((old_peak - peak) * factor)
                probs = jnp.exp2((scores - peak) * factor).astype(jnp.bfloat16)
                wide = jnp.concatenate([v_ref[:, cols], ones], axis=1)
                added = jnp.dot(probs, wide, preferred_element_type=jnp.float32)
                total_ref[head] = added if fresh else scaled + added
                peak_ref[head] = peak

        if fresh:
            one_block()
        else:
            pl.when(scalar_ref[first + number] == 1)(one_block)
    if last:
        for head in range(HEADS_HERE):
            total = total_ref[head]
            out_ref[:, head * HD : (head + 1) * HD] = (total[:, :HD] / total[:, HD:]).astype(jnp.bfloat16)


def attend(scalars, queries, first, blocks, pieces=None, state=None):
    rows, width = queries.shape
    last = state is not None
    share = rows // (NY * NXL * NC)
    tile = rows // NC
    count = len(blocks) // 2 + (1 if last else 0)
    whole = pl.BlockSpec((rows, width), lambda i, *_: (0, 0))
    state_specs = [
        pl.BlockSpec((HEADS_HERE, tile, 1), lambda i, *_: (0, i, 0)),
        pl.BlockSpec((HEADS_HERE, tile, 2 * HD), lambda i, *_: (0, i, 0)),
    ]
    in_specs = [pl.BlockSpec((NY * NXL * NC, share, width), lambda i, *_: (0, 0, 0))] + [whole] * len(blocks)
    operands = [queries.reshape(NY * NXL * NC, share, width), *blocks]
    if last:
        in_specs += [pl.BlockSpec((2, rows // NZ, width), lambda i, *_: (0, 0, 0))] * len(pieces) + state_specs
        operands += [*pieces, *state]
        out_shape = jax.ShapeDtypeStruct((rows, width), jnp.bfloat16)
        out_specs = pl.BlockSpec((tile, width), lambda i, *_: (i, 0))
        scratch = [
            pltpu.VMEM((HEADS_HERE, tile, 1), jnp.float32),
            pltpu.VMEM((HEADS_HERE, tile, 2 * HD), jnp.float32),
            pltpu.VMEM((rows, width), jnp.bfloat16),
            pltpu.VMEM((rows, width), jnp.bfloat16),
        ]
    else:
        out_shape = [
            jax.ShapeDtypeStruct((HEADS_HERE, rows, 1), jnp.float32),
            jax.ShapeDtypeStruct((HEADS_HERE, rows, 2 * HD), jnp.float32),
        ]
        out_specs, scratch = state_specs, []
    return pl.pallas_call(
        functools.partial(attend_body, count, first, last),
        out_shape=out_shape,
        grid_spec=pltpu.PrefetchScalarGridSpec(
            num_scalar_prefetch=1, grid=(NC,), in_specs=in_specs, out_specs=out_specs, scratch_shapes=scratch
        ),
        compiler_params=pltpu.CompilerParams(vmem_limit_bytes=40 * 1024 * 1024),
        cost_estimate=pl.CostEstimate(
            flops=4 * count * rows * rows * width, bytes_accessed=20 * rows * width, transcendentals=3 * count * rows * rows
        ),
    )(scalars, *operands)


def spread_clean(keys, values, root, z, xh):
    rows, width = keys.shape
    own = jnp.stack([keys.reshape(NZ, rows // NZ, width), values.reshape(NZ, rows // NZ, width)], axis=1)
    root_z = root // NXH
    distance = lax.rem(z - root_z + NZ, NZ)

    def from_device(there):
        def scatter(own):
            got = own[0]
            for step in (4, 3, 5, 2, 6, 1, 7):
                piece = lax.ppermute(own[step], "z", [(there, (there + step) % NZ)])
                got = jnp.where(distance == step, piece, got)
            return got

        return scatter

    piece = lax.switch(root_z, [from_device(there) for there in range(NZ)], own)
    piece = jnp.where(xh == lax.rem(root, NXH), piece, lax.ppermute(piece, "xh", SWAP))
    pieces = [piece]
    up = down = piece
    for number in range(4):
        up = shift(up, "z", NZ, 1)
        pieces.append(up)
        if number < 3:
            down = shift(down, "z", NZ, -1)
            pieces.append(down)
    return pieces


def project_body(kept_ref, taken_ref, own_ref, sibling_ref, out_ref):
    out_ref[...] = (
        jnp.dot(kept_ref[...], own_ref[...], preferred_element_type=jnp.float32)
        + jnp.dot(taken_ref[...], sibling_ref[...], preferred_element_type=jnp.float32)
    ).astype(jnp.bfloat16)


def project(attended, taken, own_weight, sibling_weight, low, high):
    rows, width = taken.shape
    first = low // COLUMN_TILE
    weight_spec = pl.BlockSpec((width, COLUMN_TILE), lambda i: (0, first + i))
    row_spec = pl.BlockSpec((rows, width), lambda i: (0, 0))
    return pl.pallas_call(
        project_body,
        out_shape=jax.ShapeDtypeStruct((rows, high - low), jnp.bfloat16),
        grid=((high - low) // COLUMN_TILE,),
        in_specs=[row_spec, row_spec, weight_spec, weight_spec],
        out_specs=pl.BlockSpec((rows, COLUMN_TILE), lambda i: (0, i)),
        compiler_params=pltpu.CompilerParams(vmem_limit_bytes=40 * 1024 * 1024),
        cost_estimate=pl.CostEstimate(
            flops=4 * rows * width * (high - low), bytes_accessed=6 * width * (high - low), transcendentals=0
        ),
    )(attended, taken, own_weight, sibling_weight).reshape(NXL, NY, rows // (NXL * NY), high - low)


def add(*terms):
    total = terms[0].astype(jnp.float32)
    for term in terms[1:]:
        total = total + term.astype(jnp.float32)
    return total


def sum_over_y(terms):
    half = terms[0].shape[-1] // 2
    from_below = shift(terms[2][..., :half], "y", NY, 1)
    from_above = shift(terms[2][..., half:], "y", NY, -1)
    rise = jnp.concatenate([add(terms[1][..., :half], from_below).astype(jnp.bfloat16), terms[1][..., half:]], axis=-1)
    fall = jnp.concatenate([terms[3][..., :half], add(terms[3][..., half:], from_above).astype(jnp.bfloat16)], axis=-1)
    return [terms[0], shift(rise, "y", NY, 1), shift(fall, "y", NY, -1)]


def local(queries, keys, values, residual, out_weight, gate_table, noise_steps, windows):
    z, xh, y, xl, core = (lax.axis_index(name) for name in ("z", "xh", "y", "xl", "c"))
    my_span = z * NXH + xh
    span_ids = lax.iota(jnp.int32, NZ * NXH)
    clean_root = jnp.sum(span_ids * (noise_steps == 0).astype(jnp.int32))
    rows, width = queries.shape
    share = residual.shape[0]

    lag2_keys, lag2_values = shift(keys, "z", NZ, 1), shift(values, "z", NZ, 1)
    pieces = spread_clean(keys, values, clean_root, z, xh)
    lag1_keys = lax.ppermute(jnp.where(xh == 0, keys, lag2_keys), "xh", SWAP)
    lag1_values = lax.ppermute(jnp.where(xh == 0, values, lag2_values), "xh", SWAP)
    sibling_weight = lax.ppermute(out_weight, "c", SWAP)

    scalars = jnp.stack(
        [
            jnp.int32(1),
            windows[my_span, 1],
            windows[my_span, 0],
            (my_span != clean_root).astype(jnp.int32),
            y,
            xl,
            core,
        ]
    )
    state = attend(scalars, queries, 0, [keys, values, lag2_keys, lag2_values])
    attended = attend(scalars, queries, 2, [lag1_keys, lag1_values], pieces, state)
    taken = lax.ppermute(attended[rows // 2 :], "c", SWAP)
    x_first = project(attended, taken, out_weight, sibling_weight, 0, X_FIRST)
    y_first = project(attended, taken, out_weight, sibling_weight, X_FIRST, out_weight.shape[1])

    x_got = lax.ppermute(x_first[1], "xl", SWAP)
    here = sum_over_y([y_first[:, number] for number in range(NY)])
    here_kept = [term[0] for term in here]
    here_sent = add(*[term[1] for term in here]).astype(jnp.bfloat16)
    here_got = lax.ppermute(here_sent, "xl", SWAP)
    x_sum = add(x_first[0], x_got).astype(jnp.bfloat16)
    left = add(*sum_over_y([x_sum[number] for number in range(NY)]))
    right = add(*here_kept, here_got)
    gate_row = lax.dynamic_slice_in_dim(gate_table, noise_steps[my_span], 1, 0)
    summed = jnp.concatenate([left, right], axis=1)
    return (residual.astype(jnp.float32) + gate_row * summed).astype(jnp.bfloat16)


def solution(mesh):
    fine = Mesh(mesh.devices.reshape(NZ, NXH, NY, NXL, NC), ("z", "xh", "y", "xl", "c"))
    span, mp = ("z", "xh"), ("y", "xl", "c")
    in_specs = (
        P(span, mp),
        P(span, mp),
        P(span, mp),
        P(span + mp, None),
        P(mp, None),
        P(),
        P(),
        P(),
    )
    out_specs = P(span + mp, None)
    return jax.shard_map(local, mesh=fine, in_specs=in_specs, out_specs=out_specs, check_vma=False)
```

```python
import functools
import math

import jax
import jax.numpy as jnp
from jax import lax
from jax.experimental import pallas as pl
from jax.experimental.pallas import tpu as pltpu
from jax.sharding import Mesh, PartitionSpec as P

HD = 128
HEADS_HERE = 3
NZ, NXH, NY, NXL, NC = 8, 2, 4, 2, 2
X_FIRST = 2688
CHUNK = 16
LOG2E = math.log2(math.e)
SWAP = [(0, 1), (1, 0)]


def shift(value, axis, count, steps):
    return lax.ppermute(value, axis, [(i, (i + steps) % count) for i in range(count)])


def attend_body(fresh, last, flags, *refs):
    refs = list(refs)
    scalar_ref, q_ref = refs.pop(0), refs.pop(0)
    scores_ref, probs_ref = refs.pop(), refs.pop()
    if last:
        clean = (refs.pop(), refs.pop())
        peak_ref, total_ref, out_ref = refs.pop(), refs.pop(), refs.pop()
    else:
        total_ref, peak_ref = refs.pop(), refs.pop()
    if not fresh:
        old_total_ref, old_peak_ref = refs.pop(), refs.pop()
        peak_ref[...] = old_peak_ref[...]
        total_ref[...] = old_total_ref[...]
    if last:
        pieces = refs
        piece_rows = pieces[0].shape[1]

        @pl.when(pl.program_id(0) == 0)
        def _():
            for number, piece in enumerate(pieces):
                for side in range(2):
                    clean[side][pl.ds(number * piece_rows, piece_rows)] = piece[side]

        blocks = [clean]
    else:
        blocks = list(zip(refs[::2], refs[1::2]))
    factor = HD ** (-0.5) * LOG2E
    tile = probs_ref.shape[1]
    ones = jnp.ones((blocks[0][0].shape[0], HD), jnp.bfloat16)
    y, xl, core = scalar_ref[4], scalar_ref[5], scalar_ref[6]
    places = []
    for xl_step in range(NXL):
        for y_step in range(NY):
            y_there = lax.rem(y + y_step, NY)
            xl_there = lax.rem(xl + xl_step, NXL)
            places.append((y_there * NXL + xl_there) * NC + lax.rem(core + pl.program_id(0), NC))

    def one_block(first, k_ref, v_ref):
        def take_scores(head):
            cols = slice(head * HD, (head + 1) * HD)
            rows = jnp.concatenate([q_ref[place, :, cols] for place in places], axis=0)
            scores_ref[head % 2] = lax.dot_general(
                rows, k_ref[:, cols], (((1,), (1,)), ((), ())), preferred_element_type=jnp.float32
            )

        take_scores(0)
        for head in range(HEADS_HERE):
            cols = slice(head * HD, (head + 1) * HD)
            if head + 1 < HEADS_HERE:
                take_scores(head + 1)
            scales = []
            for low in range(0, tile, CHUNK):
                rows = slice(low, low + CHUNK)
                scores = scores_ref[head % 2, rows]
                peak = jnp.max(scores, axis=1, keepdims=True)
                if not first:
                    old_peak = peak_ref[head, rows]
                    peak = jnp.maximum(old_peak, peak)
                    scales.append(jnp.exp2((old_peak - peak) * factor))
                probs_ref[head % 2, rows] = jnp.exp2(((scores - peak) * factor).astype(jnp.bfloat16))
                peak_ref[head, rows] = peak
            wide = jnp.concatenate([v_ref[:, cols], ones], axis=1)
            added = jnp.dot(probs_ref[head % 2], wide, preferred_element_type=jnp.float32)
            total_ref[head] = added if first else total_ref[head] * jnp.concatenate(scales, axis=0) + added

    for number, (k_ref, v_ref) in enumerate(blocks):
        if fresh and number == 0:
            one_block(True, k_ref, v_ref)
        else:
            pl.when(scalar_ref[flags[number]] == 1)(functools.partial(one_block, False, k_ref, v_ref))
    if last:
        for head in range(HEADS_HERE):
            total = total_ref[head]
            out_ref[:, head * HD : (head + 1) * HD] = (total[:, :HD] / total[:, HD:]).astype(jnp.bfloat16)


def attend(scalars, queries, flags, blocks, state=None, last=False):
    rows, width = queries.shape
    fresh = state is None
    share = rows // (NY * NXL * NC)
    tile = rows // NC
    count = len(flags)
    state_specs = [
        pl.BlockSpec((HEADS_HERE, tile, 1), lambda i, *_: (0, i, 0)),
        pl.BlockSpec((HEADS_HERE, tile, 2 * HD), lambda i, *_: (0, i, 0)),
    ]
    in_specs = [pl.BlockSpec((NY * NXL * NC, share, width), lambda i, *_: (0, 0, 0))]
    in_specs += [pl.BlockSpec(block.shape, lambda i, *_, rank=block.ndim: (0,) * rank) for block in blocks]
    operands = [queries.reshape(NY * NXL * NC, share, width), *blocks]
    if not fresh:
        in_specs += state_specs
        operands += state
    scratch = [pltpu.VMEM((2, tile, rows), jnp.bfloat16), pltpu.VMEM((2, tile, rows), jnp.float32)]
    if last:
        out_shape = jax.ShapeDtypeStruct((rows, width), jnp.bfloat16)
        out_specs = pl.BlockSpec((tile, width), lambda i, *_: (i, 0))
        scratch = [
            pltpu.VMEM((HEADS_HERE, tile, 2 * HD), jnp.float32),
            pltpu.VMEM((HEADS_HERE, tile, 1), jnp.float32),
            pltpu.VMEM((rows, width), jnp.bfloat16),
            pltpu.VMEM((rows, width), jnp.bfloat16),
        ] + scratch
    else:
        out_shape = [
            jax.ShapeDtypeStruct((HEADS_HERE, rows, 1), jnp.float32),
            jax.ShapeDtypeStruct((HEADS_HERE, rows, 2 * HD), jnp.float32),
        ]
        out_specs = state_specs
    return pl.pallas_call(
        functools.partial(attend_body, fresh, last, flags),
        out_shape=out_shape,
        grid_spec=pltpu.PrefetchScalarGridSpec(
            num_scalar_prefetch=1, grid=(NC,), in_specs=in_specs, out_specs=out_specs, scratch_shapes=scratch
        ),
        compiler_params=pltpu.CompilerParams(vmem_limit_bytes=40 * 1024 * 1024),
        cost_estimate=pl.CostEstimate(
            flops=4 * count * rows * rows * width, bytes_accessed=20 * rows * width, transcendentals=3 * count * rows * rows
        ),
    )(scalars, *operands)


def spread_clean(keys, values, root, z, xh, beside):
    rows, width = keys.shape
    own = jnp.stack([keys.reshape(NZ, rows // NZ, width), values.reshape(NZ, rows // NZ, width)], axis=1)
    distance = lax.rem(z - root // NXH + NZ, NZ)
    at_root = distance == 0
    beside = list(beside)
    up, down = own[4], own[5]
    for number in range(4):
        up = shift(jnp.where(at_root, own[4 - number], up) if number else up, "z", NZ, 1)
        if number < 3:
            down = shift(jnp.where(at_root, own[5 + number], down) if number else down, "z", NZ, -1)
        if number % 2:
            up, beside[number // 2] = lax.optimization_barrier((up, beside[number // 2]))
    piece = jnp.where(at_root, own[0], jnp.where(distance <= 4, up, down))
    piece = jnp.where(xh == lax.rem(root, NXH), piece, lax.ppermute(piece, "xh", SWAP))
    pieces = [piece]
    up = down = piece
    for number in range(4):
        up = shift(up, "z", NZ, 1)
        pieces.append(up)
        if number < 3:
            down = shift(down, "z", NZ, -1)
            pieces.append(down)
    return pieces, beside


def add(*terms):
    total = terms[0].astype(jnp.float32)
    for term in terms[1:]:
        total = total + term.astype(jnp.float32)
    return total


def sum_over_y(terms):
    half = terms[0].shape[-1] // 2
    from_below = shift(terms[2][..., :half], "y", NY, 1)
    from_above = shift(terms[2][..., half:], "y", NY, -1)
    rise = jnp.concatenate([add(terms[1][..., :half], from_below).astype(jnp.bfloat16), terms[1][..., half:]], axis=-1)
    fall = jnp.concatenate([terms[3][..., :half], add(terms[3][..., half:], from_above).astype(jnp.bfloat16)], axis=-1)
    return [terms[0], shift(rise, "y", NY, 1), shift(fall, "y", NY, -1)]


def local(queries, keys, values, residual, out_weight, gate_table, noise_steps, windows):
    z, xh, y, xl, core = (lax.axis_index(name) for name in ("z", "xh", "y", "xl", "c"))
    my_span = z * NXH + xh
    span_ids = lax.iota(jnp.int32, NZ * NXH)
    clean_root = jnp.sum(span_ids * (noise_steps == 0).astype(jnp.int32))
    rows, width = queries.shape
    share = residual.shape[0]

    beside = [shift(keys, "z", NZ, 1), shift(values, "z", NZ, 1)]
    pieces, (lag2_keys, lag2_values) = spread_clean(keys, values, clean_root, z, xh, beside)
    lag1_keys = lax.ppermute(jnp.where(xh == 0, keys, lag2_keys), "xh", SWAP)
    lag1_values = lax.ppermute(jnp.where(xh == 0, values, lag2_values), "xh", SWAP)
    weight = jnp.concatenate([out_weight, lax.ppermute(out_weight, "c", SWAP)], axis=0)

    scalars = jnp.stack(
        [
            jnp.int32(1),
            windows[my_span, 1],
            windows[my_span, 0],
            (my_span != clean_root).astype(jnp.int32),
            y,
            xl,
            core,
        ]
    )
    state = attend(scalars, queries, (0, 1), [keys, values, lag2_keys, lag2_values])
    state = attend(scalars, queries, (2,), [lag1_keys, lag1_values], state)
    state, weight = lax.optimization_barrier((state, weight))
    attended = attend(scalars, queries, (3,), pieces, state, last=True)
    taken = lax.ppermute(attended[rows // 2 :], "c", SWAP)
    both = jnp.concatenate([attended[: rows // 2], taken], axis=1)

    def project(low, high):
        terms = jnp.dot(both, weight[:, low:high], preferred_element_type=jnp.float32).astype(jnp.bfloat16)
        return terms.reshape(NXL, NY, share, high - low)

    x_first = project(0, X_FIRST)
    y_first = project(X_FIRST, out_weight.shape[1])

    x_got = lax.ppermute(x_first[1], "xl", SWAP)
    here = sum_over_y([y_first[:, number] for number in range(NY)])
    here_kept = [term[0] for term in here]
    here_sent = add(*[term[1] for term in here]).astype(jnp.bfloat16)
    here_got = lax.ppermute(here_sent, "xl", SWAP)
    x_sum = add(x_first[0], x_got).astype(jnp.bfloat16)
    left = add(*sum_over_y([x_sum[number] for number in range(NY)]))
    right = add(*here_kept, here_got)
    gate_row = lax.dynamic_slice_in_dim(gate_table, noise_steps[my_span], 1, 0)
    summed = jnp.concatenate([left, right], axis=1)
    return (residual.astype(jnp.float32) + gate_row * summed).astype(jnp.bfloat16)


def solution(mesh):
    fine = Mesh(mesh.devices.reshape(NZ, NXH, NY, NXL, NC), ("z", "xh", "y", "xl", "c"))
    span, mp = ("z", "xh"), ("y", "xl", "c")
    in_specs = (
        P(span, mp),
        P(span, mp),
        P(span, mp),
        P(span + mp, None),
        P(mp, None),
        P(),
        P(),
        P(),
    )
    out_specs = P(span + mp, None)
    return jax.shard_map(local, mesh=fine, in_specs=in_specs, out_specs=out_specs, check_vma=False)
```

```python
import functools
import math

import jax
import jax.numpy as jnp
from jax import lax
from jax.experimental import pallas as pl
from jax.experimental.pallas import tpu as pltpu
from jax.sharding import Mesh, PartitionSpec as P

HD = 128
HEADS_HERE = 3
NZ, NXH, NY, NXL, NC = 8, 2, 4, 2, 2
X_FIRST = 2688
CHUNK = 16
UP = 2
OWN, LAG1, LAG2, CLEAN = range(4)
LAGS_BACK = {LAG1: 1, LAG2: 2}
LOG2E = math.log2(math.e)
SWAP = [(0, 1), (1, 0)]


def shift(value, axis, count, steps):
    return lax.ppermute(value, axis, [(i, (i + steps) % count) for i in range(count)])


def attend_body(block, base, noise_ref, windows_ref, q_ref, *refs):
    first, last = block == OWN, block == CLEAN
    refs = list(refs)
    scores_ref, probs_ref = refs.pop(), refs.pop()
    if last:
        clean = (refs.pop(), refs.pop())
        total_ref, out_ref = refs.pop(), refs.pop()
        peak_ref = None
    else:
        total_ref, peak_ref = refs.pop(), refs.pop()
    if not first:
        old_total_ref, old_peak_ref = refs.pop(), refs.pop()
    if last:
        piece_rows = refs[0].shape[1]

        for number, piece in enumerate(refs):
            for side in range(2):
                clean[side][pl.ds(number * piece_rows, piece_rows)] = piece[side]

        k_ref, v_ref = clean
    else:
        k_ref, v_ref = refs
    factor = HD ** (-0.5) * LOG2E
    group = probs_ref.shape[1]
    ones = jnp.ones((k_ref.shape[0], HD), jnp.bfloat16)
    y, xl, core = (lax.axis_index(name) for name in ("y", "xl", "c"))
    span = lax.axis_index("z") * NXH + lax.axis_index("xh")
    core = lax.rem(core + base + pl.program_id(0), NC)
    places = []
    for xl_step in range(NXL):
        for y_step in range(NY):
            places.append((lax.rem(y + y_step, NY) * NXL + lax.rem(xl + xl_step, NXL)) * NC + core)
    share = q_ref.shape[1]
    places_each = group // share
    units = [(head, part) for head in range(HEADS_HERE) for part in range(len(places) // places_each)]

    def compute():
        def take_scores(unit):
            head, part = units[unit]
            cols = slice(head * HD, (head + 1) * HD)
            held = places[part * places_each : (part + 1) * places_each]
            rows = jnp.concatenate([q_ref[place, :, cols] for place in held], axis=0)
            scores_ref[unit % 2] = lax.dot_general(
                rows, k_ref[:, cols], (((1,), (1,)), ((), ())), preferred_element_type=jnp.float32
            )

        take_scores(0)
        for unit, (head, part) in enumerate(units):
            cols = slice(head * HD, (head + 1) * HD)
            start = part * group
            if unit + 1 < len(units):
                take_scores(unit + 1)
            scales = []
            for low in range(0, group, CHUNK):
                rows = slice(low, low + CHUNK)
                there = slice(start + low, start + low + CHUNK)
                scores = scores_ref[unit % 2, rows]
                peak = jnp.max(scores, axis=1, keepdims=True)
                if not first:
                    old_peak = old_peak_ref[head, there]
                    peak = jnp.maximum(old_peak, peak)
                    scales.append(jnp.exp2((old_peak - peak) * factor))
                probs_ref[unit % 2, rows] = jnp.exp2(((scores - peak) * factor).astype(jnp.bfloat16))
                if not last:
                    peak_ref[head, there] = peak
            wide = jnp.concatenate([v_ref[:, cols], ones], axis=1)
            added = jnp.dot(probs_ref[unit % 2], wide, preferred_element_type=jnp.float32)
            there = slice(start, start + group)
            total_ref[head, there] = added if first else old_total_ref[head, there] * jnp.concatenate(scales, axis=0) + added

    if first:
        compute()
    else:
        if last:
            live = noise_ref[span] != 0
        else:
            live = windows_ref[span, LAGS_BACK[block] - 1] == 1
        pl.when(live)(compute)

        @pl.when(jnp.logical_not(live))
        def _():
            total_ref[...] = old_total_ref[...]
            if not last:
                peak_ref[...] = old_peak_ref[...]

    if last:
        for head in range(HEADS_HERE):
            total = total_ref[head]
            out_ref[:, head * HD : (head + 1) * HD] = (total[:, :HD] / total[:, HD:]).astype(jnp.bfloat16)


def attend(block, noise_steps, windows, queries, arrays, state=(), halves=(0, 1)):
    rows, width = queries.shape
    share = rows // (NY * NXL * NC)
    tile = rows // NC
    group = tile // 2
    state_specs = [
        pl.BlockSpec((HEADS_HERE, tile, 1), lambda i, *_: (0, i + halves[0], 0)),
        pl.BlockSpec((HEADS_HERE, tile, 2 * HD), lambda i, *_: (0, i + halves[0], 0)),
    ]
    in_specs = [pl.BlockSpec((NY * NXL * NC, share, width), lambda i, *_: (0, 0, 0))]
    in_specs += [pl.BlockSpec(array.shape, lambda i, *_, rank=array.ndim: (0,) * rank) for array in arrays]
    in_specs += state_specs[: len(state)]
    scratch = [pltpu.VMEM((2, group, rows), jnp.bfloat16), pltpu.VMEM((2, group, rows), jnp.float32)]
    if block == CLEAN:
        out_shape = jax.ShapeDtypeStruct((tile * len(halves), width), jnp.bfloat16)
        out_specs = pl.BlockSpec((tile, width), lambda i, *_: (i, 0))
        scratch = [
            pltpu.VMEM((HEADS_HERE, tile, 2 * HD), jnp.float32),
            pltpu.VMEM((rows, width), jnp.bfloat16),
            pltpu.VMEM((rows, width), jnp.bfloat16),
        ] + scratch
    else:
        out_shape = [
            jax.ShapeDtypeStruct((HEADS_HERE, rows, 1), jnp.float32),
            jax.ShapeDtypeStruct((HEADS_HERE, rows, 2 * HD), jnp.float32),
        ]
        out_specs = state_specs
    return pl.pallas_call(
        functools.partial(attend_body, block, halves[0]),
        out_shape=out_shape,
        grid_spec=pltpu.PrefetchScalarGridSpec(
            num_scalar_prefetch=2, grid=(len(halves),), in_specs=in_specs, out_specs=out_specs, scratch_shapes=scratch
        ),
        compiler_params=pltpu.CompilerParams(vmem_limit_bytes=40 * 1024 * 1024),
        cost_estimate=pl.CostEstimate(
            flops=2 * len(halves) * rows * rows * width, bytes_accessed=20 * rows * width, transcendentals=3 * rows * rows
        ),
    )(noise_steps, windows, queries.reshape(NY * NXL * NC, share, width), *arrays, *state)


def fetch(keys, values, root, z, xh, weight):
    rows, width = keys.shape
    cut = rows // NZ

    def own(number):
        part = slice(number * cut, (number + 1) * cut)
        return jnp.stack([keys[part], values[part]])

    distance = lax.rem(z - root // NXH + NZ, NZ)
    at_root = distance == 0
    lag2_keys = shift(keys, "z", NZ, 1)
    down = own(UP + 1)
    for number in range(UP + 1, NZ):
        if number == UP + 3:
            down, lag2_keys, weight = lax.optimization_barrier((down, lag2_keys, weight))
        down = shift(jnp.where(at_root, own(number), down) if number > UP + 1 else down, "z", NZ, -1)
    lag1_keys = lax.ppermute(jnp.where(xh == 0, keys, lag2_keys), "xh", SWAP)
    up, _ = lax.optimization_barrier((own(UP), lag2_keys))
    for number in range(UP, 0, -1):
        up = shift(jnp.where(at_root, own(number), up) if number < UP else up, "z", NZ, 1)
    values_late, up = lax.optimization_barrier((values, up))
    lag2_values = shift(values_late, "z", NZ, 1)
    piece = jnp.where(at_root, own(0), jnp.where(distance <= UP, up, down))
    piece, lag1_keys = lax.optimization_barrier((piece, lag1_keys))
    piece = jnp.where(xh == lax.rem(root, NXH), piece, lax.ppermute(piece, "xh", SWAP))
    piece, lag2_values = lax.optimization_barrier((piece, lag2_values))
    lag1_values = lax.ppermute(jnp.where(xh == 0, values, lag2_values), "xh", SWAP)
    pieces = [piece]
    up = down = piece
    for number in range(4):
        up = shift(up, "z", NZ, 1)
        pieces.append(up)
        if number < 3:
            down = shift(down, "z", NZ, -1)
            pieces.append(down)
    return [lag2_keys, lag2_values], [lag1_keys, lag1_values], pieces, weight


def add(*terms):
    total = terms[0].astype(jnp.float32)
    for term in terms[1:]:
        total = total + term.astype(jnp.float32)
    return total


def sum_over_y(terms):
    half = terms[0].shape[-1] // 2
    from_below = shift(terms[2][..., :half], "y", NY, 1)
    from_above = shift(terms[2][..., half:], "y", NY, -1)
    rise = jnp.concatenate([add(terms[1][..., :half], from_below).astype(jnp.bfloat16), terms[1][..., half:]], axis=-1)
    fall = jnp.concatenate([terms[3][..., :half], add(terms[3][..., half:], from_above).astype(jnp.bfloat16)], axis=-1)
    return [terms[0], shift(rise, "y", NY, 1), shift(fall, "y", NY, -1)]


def local(queries, keys, values, residual, out_weight, gate_table, noise_steps, windows):
    z, xh = lax.axis_index("z"), lax.axis_index("xh")
    my_span = z * NXH + xh
    span_ids = lax.iota(jnp.int32, NZ * NXH)
    clean_root = jnp.sum(span_ids * (noise_steps == 0).astype(jnp.int32))
    rows, width = queries.shape
    share = residual.shape[0]

    weight = jnp.concatenate([out_weight, lax.ppermute(out_weight, "c", SWAP)], axis=0)
    lag2, lag1, pieces, weight = fetch(keys, values, clean_root, z, xh, weight)
    state = attend(OWN, noise_steps, windows, queries, [keys, values])
    state = attend(LAG2, noise_steps, windows, queries, lag2, state)
    state = attend(LAG1, noise_steps, windows, queries, lag1, state)
    given = attend(CLEAN, noise_steps, windows, queries, pieces, state, halves=(1,))
    taken = lax.ppermute(given, "c", SWAP)
    kept = attend(CLEAN, noise_steps, windows, queries, pieces, state, halves=(0,))
    both = jnp.concatenate([kept, taken], axis=1)

    def project(low, high):
        terms = jnp.dot(both, weight[:, low:high], preferred_element_type=jnp.float32).astype(jnp.bfloat16)
        return terms.reshape(NXL, NY, share, high - low)

    x_first = project(0, X_FIRST)
    y_first = project(X_FIRST, out_weight.shape[1])

    x_got = lax.ppermute(x_first[1], "xl", SWAP)
    here = sum_over_y([y_first[:, number] for number in range(NY)])
    here_kept = [term[0] for term in here]
    here_sent = add(*[term[1] for term in here]).astype(jnp.bfloat16)
    here_got = lax.ppermute(here_sent, "xl", SWAP)
    x_sum = add(x_first[0], x_got).astype(jnp.bfloat16)
    left = add(x_sum[0], *[shift(x_sum[step], "y", NY, step) for step in (1, 3, 2)])
    right = add(*here_kept, here_got)
    gate_row = lax.dynamic_slice_in_dim(gate_table, noise_steps[my_span], 1, 0)
    summed = jnp.concatenate([left, right], axis=1)
    return (residual.astype(jnp.float32) + gate_row * summed).astype(jnp.bfloat16)


def solution(mesh):
    fine = Mesh(mesh.devices.reshape(NZ, NXH, NY, NXL, NC), ("z", "xh", "y", "xl", "c"))
    span, mp = ("z", "xh"), ("y", "xl", "c")
    in_specs = (
        P(span, mp),
        P(span, mp),
        P(span, mp),
        P(span + mp, None),
        P(mp, None),
        P(),
        P(),
        P(),
    )
    out_specs = P(span + mp, None)
    return jax.shard_map(local, mesh=fine, in_specs=in_specs, out_specs=out_specs, check_vma=False)
```

```python
import functools
import math

import jax
import jax.numpy as jnp
from jax import lax
from jax.experimental import pallas as pl
from jax.experimental.pallas import tpu as pltpu
from jax.sharding import Mesh, PartitionSpec as P

HD = 128
HEADS_HERE = 3
NZ, NXH, NY, NXL, NC = 8, 2, 4, 2, 2
X_FIRST = 2560
CHUNK = 16
UP = 2
OWN, LAG1, LAG2, CLEAN = range(4)
LIVE = 3
LOG2E = math.log2(math.e)
SWAP = [(0, 1), (1, 0)]


def shift(value, axis, count, steps):
    return lax.ppermute(value, axis, [(i, (i + steps) % count) for i in range(count)])


def attend_body(blocks, base, scalar_ref, q_ref, *refs):
    last = blocks[-1] == CLEAN
    refs = list(refs)
    scores_ref, probs_ref = refs.pop(), refs.pop()
    if last:
        v_clean, k_clean, out_ref = refs.pop(), refs.pop(), refs.pop()
    else:
        state_ref = refs.pop()
    if blocks[0] != OWN:
        old_ref = refs.pop()
    if last:
        cut = refs[0].shape[1]
        for number, piece in enumerate(refs):
            k_clean[pl.ds(number * cut, cut)] = piece[0]
            v_clean[pl.ds(number * cut, cut)] = piece[1]
        refs = [k_clean, v_clean]
    factor = HD ** (-0.5) * LOG2E
    group = probs_ref.shape[1]
    ones = jnp.ones((refs[0].shape[0], HD), jnp.bfloat16)
    in_sum = lax.broadcasted_iota(jnp.int32, (group, HD), 1) < HD // 2
    y, xl = scalar_ref[1], scalar_ref[2]
    core = lax.rem(scalar_ref[3] + base + pl.program_id(0), NC)
    places = []
    for xl_step in range(NXL):
        for y_step in range(NY):
            places.append((lax.rem(y + y_step, NY) * NXL + lax.rem(xl + xl_step, NXL)) * NC + core)
    places_each = group // q_ref.shape[1]
    units = [(head, part) for head in range(HEADS_HERE) for part in range(len(places) // places_each)]

    def compute(k_ref, v_ref, from_ref):
        def take_scores(unit):
            head, part = units[unit]
            cols = slice(head * HD, (head + 1) * HD)
            held = places[part * places_each : (part + 1) * places_each]
            rows = jnp.concatenate([q_ref[place, :, cols] for place in held], axis=0)
            scores_ref[unit % 2] = lax.dot_general(
                rows, k_ref[:, cols], (((1,), (1,)), ((), ())), preferred_element_type=jnp.float32
            )

        take_scores(0)
        for unit, (head, part) in enumerate(units):
            cols = slice(head * HD, (head + 1) * HD)
            start = part * group
            if unit + 1 < len(units):
                take_scores(unit + 1)
            scales, peaks = [], []
            for low in range(0, group, CHUNK):
                rows = slice(low, low + CHUNK)
                scores = scores_ref[unit % 2, rows]
                peak = jnp.max(scores, axis=1, keepdims=True)
                if from_ref is not None:
                    old_peak = from_ref[head, start + low : start + low + CHUNK, 2 * HD - 1 :]
                    peak = jnp.maximum(old_peak, peak)
                    scales.append(jnp.exp2((old_peak - peak) * factor))
                probs_ref[unit % 2, rows] = jnp.exp2(((scores - peak) * factor).astype(jnp.bfloat16))
                peaks.append(peak)
            wide = jnp.concatenate([v_ref[:, cols], ones], axis=1)
            added = jnp.dot(probs_ref[unit % 2], wide, preferred_element_type=jnp.float32)
            there = slice(start, start + group)
            if from_ref is not None:
                added = from_ref[head, there] * jnp.concatenate(scales, axis=0) + added
            if last:
                out_ref[there, cols] = (added[:, :HD] / added[:, HD : HD + 1]).astype(jnp.bfloat16)
            else:
                state_ref[head, there, :HD] = added[:, :HD]
                state_ref[head, there, HD:] = jnp.where(in_sum, added[:, HD:], jnp.concatenate(peaks, axis=0))

    for number, block in enumerate(blocks):
        k_ref, v_ref = refs[2 * number : 2 * number + 2]
        if block == OWN:
            compute(k_ref, v_ref, None)
            continue
        live = scalar_ref[LIVE + block] == 1
        from_ref = state_ref if number else old_ref
        pl.when(live)(functools.partial(compute, k_ref, v_ref, from_ref))
        if number == 0:

            @pl.when(jnp.logical_not(live))
            def _():
                if last:
                    for head in range(HEADS_HERE):
                        cols = slice(head * HD, (head + 1) * HD)
                        out_ref[:, cols] = (old_ref[head, :, :HD] / old_ref[head, :, HD : HD + 1]).astype(jnp.bfloat16)
                else:
                    state_ref[...] = old_ref[...]


def attend(blocks, scalars, queries, arrays, state=(), halves=(0, 1)):
    rows, width = queries.shape
    share = rows // (NY * NXL * NC)
    tile = rows // NC
    group = tile // 2
    state_spec = pl.BlockSpec((HEADS_HERE, tile, 2 * HD), lambda i, *_: (0, i + halves[0], 0))
    in_specs = [pl.BlockSpec((NY * NXL * NC, share, width), lambda i, *_: (0, 0, 0))]
    in_specs += [pl.BlockSpec(array.shape, lambda i, *_, rank=array.ndim: (0,) * rank) for array in arrays]
    in_specs += [state_spec] * len(state)
    scratch = [pltpu.VMEM((2, group, rows), jnp.bfloat16), pltpu.VMEM((2, group, rows), jnp.float32)]
    if blocks[-1] == CLEAN:
        out_shape = jax.ShapeDtypeStruct((tile * len(halves), width), jnp.bfloat16)
        out_specs = pl.BlockSpec((tile, width), lambda i, *_: (i, 0))
        scratch = [pltpu.VMEM((rows, width), jnp.bfloat16)] * 2 + scratch
    else:
        out_shape = jax.ShapeDtypeStruct((HEADS_HERE, rows, 2 * HD), jnp.float32)
        out_specs = state_spec
    work = len(halves) * len(blocks) * rows * rows
    return pl.pallas_call(
        functools.partial(attend_body, blocks, halves[0]),
        out_shape=out_shape,
        grid_spec=pltpu.PrefetchScalarGridSpec(
            num_scalar_prefetch=1, grid=(len(halves),), in_specs=in_specs, out_specs=out_specs, scratch_shapes=scratch
        ),
        compiler_params=pltpu.CompilerParams(vmem_limit_bytes=40 * 1024 * 1024),
        cost_estimate=pl.CostEstimate(flops=2 * work * width, bytes_accessed=20 * rows * width, transcendentals=2 * work),
    )(scalars, queries.reshape(NY * NXL * NC, share, width), *arrays, *state)


def fetch(keys, values, root, z, xh, own_pass):
    rows, width = keys.shape
    cut = rows // NZ

    pieces = jnp.stack([keys.reshape(NZ, cut, width), values.reshape(NZ, cut, width)], axis=1)

    def own(number):
        return pieces[number]

    distance = lax.rem(z - root // NXH + NZ, NZ)
    at_root = distance == 0
    lag2_keys = shift(keys, "z", NZ, 1)
    down = own(UP + 1)
    for number in range(UP + 1, NZ):
        if number == UP + 3:
            down, lag2_keys, own_pass = lax.optimization_barrier((down, lag2_keys, own_pass))
        down = shift(jnp.where(at_root, own(number), down) if number > UP + 1 else down, "z", NZ, -1)
    lag1_keys = lax.ppermute(jnp.where(xh == 0, keys, lag2_keys), "xh", SWAP)
    up, _ = lax.optimization_barrier((own(UP), lag2_keys))
    for number in range(UP, 0, -1):
        up = shift(jnp.where(at_root, own(number), up) if number < UP else up, "z", NZ, 1)
    values_late, up = lax.optimization_barrier((values, up))
    lag2_values = shift(values_late, "z", NZ, 1)
    piece = jnp.where(at_root, own(0), jnp.where(distance <= UP, up, down))
    piece, lag1_keys = lax.optimization_barrier((piece, lag1_keys))
    piece = jnp.where(xh == lax.rem(root, NXH), piece, lax.ppermute(piece, "xh", SWAP))
    piece, lag2_values = lax.optimization_barrier((piece, lag2_values))
    lag1_values = lax.ppermute(jnp.where(xh == 0, values, lag2_values), "xh", SWAP)
    gathered = [piece]
    up = down = piece
    for number in range(4):
        up = shift(up, "z", NZ, 1)
        gathered.append(up)
        if number < 3:
            down = shift(down, "z", NZ, -1)
            gathered.append(down)
    return own_pass, [lag2_keys, lag2_values, lag1_keys, lag1_values], gathered


def add(*terms):
    total = terms[0].astype(jnp.float32)
    for term in terms[1:]:
        total = total + term.astype(jnp.float32)
    return total


def sum_over_y(terms):
    half = terms[0].shape[-1] // 2
    from_below = shift(terms[2][..., :half], "y", NY, 1)
    from_above = shift(terms[2][..., half:], "y", NY, -1)
    rise = jnp.concatenate([add(terms[1][..., :half], from_below).astype(jnp.bfloat16), terms[1][..., half:]], axis=-1)
    fall = jnp.concatenate([terms[3][..., :half], add(terms[3][..., half:], from_above).astype(jnp.bfloat16)], axis=-1)
    return [terms[0], shift(rise, "y", NY, 1), shift(fall, "y", NY, -1)]


def local(queries, keys, values, residual, out_weight, gate_table, noise_steps, windows):
    z, xh, y, xl, core = (lax.axis_index(name) for name in ("z", "xh", "y", "xl", "c"))
    my_span = z * NXH + xh
    span_ids = lax.iota(jnp.int32, NZ * NXH)
    clean_root = jnp.sum(span_ids * (noise_steps == 0).astype(jnp.int32))
    rows, width = queries.shape
    share = residual.shape[0]

    scalars = jnp.stack(
        [
            jnp.int32(1),
            y,
            xl,
            core,
            windows[my_span, 0],
            windows[my_span, 1],
            (my_span != clean_root).astype(jnp.int32),
        ]
    )
    sibling_weight = lax.ppermute(out_weight, "c", SWAP)
    state = attend((OWN,), scalars, queries, [keys, values])
    state, lags, pieces = fetch(keys, values, clean_root, z, xh, state)
    state = attend((LAG2, LAG1), scalars, queries, lags, [state])
    given = attend((CLEAN,), scalars, queries, pieces, [state], halves=(1,))
    taken = lax.ppermute(given, "c", SWAP)
    kept = attend((CLEAN,), scalars, queries, pieces, [state], halves=(0,))

    def project(taken, low, high):
        terms = jnp.dot(kept, out_weight[:, low:high], preferred_element_type=jnp.float32)
        terms = terms + jnp.dot(taken, sibling_weight[:, low:high], preferred_element_type=jnp.float32)
        return terms.astype(jnp.bfloat16).reshape(NXL, NY, share, high - low)

    x_first = project(taken, 0, X_FIRST)
    y_first = project(taken, X_FIRST, out_weight.shape[1])

    x_got = lax.ppermute(x_first[1], "xl", SWAP)
    here = sum_over_y([y_first[:, number] for number in range(NY)])
    here_kept = [term[0] for term in here]
    here_sent = add(*[term[1] for term in here]).astype(jnp.bfloat16)
    here_got = lax.ppermute(here_sent, "xl", SWAP)
    x_sum = add(x_first[0], x_got).astype(jnp.bfloat16)
    left = add(*sum_over_y([x_sum[number] for number in range(NY)]))
    right = add(*here_kept, here_got)
    gate_row = lax.dynamic_slice_in_dim(gate_table, noise_steps[my_span], 1, 0)
    summed = jnp.concatenate([left, right], axis=1)
    return (residual.astype(jnp.float32) + gate_row * summed).astype(jnp.bfloat16)


def solution(mesh):
    fine = Mesh(mesh.devices.reshape(NZ, NXH, NY, NXL, NC), ("z", "xh", "y", "xl", "c"))
    span, mp = ("z", "xh"), ("y", "xl", "c")
    in_specs = (
        P(span, mp),
        P(span, mp),
        P(span, mp),
        P(span + mp, None),
        P(mp, None),
        P(),
        P(),
        P(),
    )
    out_specs = P(span + mp, None)
    return jax.shard_map(local, mesh=fine, in_specs=in_specs, out_specs=out_specs, check_vma=False)
```

```python
import functools
import math

import jax
import jax.numpy as jnp
from jax import lax
from jax.experimental import pallas as pl
from jax.experimental.pallas import tpu as pltpu
from jax.sharding import Mesh, PartitionSpec as P

HD = 128
HEADS_HERE = 3
NZ, NXH, NY, NXL, NC = 8, 2, 4, 2, 2
X_FIRST = 2688
CHUNK = 16
LOG2E = math.log2(math.e)
SWAP = [(0, 1), (1, 0)]


def shift(value, axis, count, steps):
    return lax.ppermute(value, axis, [(i, (i + steps) % count) for i in range(count)])


def attend_body(fresh, last, flags, *refs):
    refs = list(refs)
    scalar_ref, q_ref = refs.pop(0), refs.pop(0)
    scores_ref, probs_ref = refs.pop(), refs.pop()
    if last:
        clean = (refs.pop(), refs.pop())
        peak_ref, total_ref, out_ref = refs.pop(), refs.pop(), refs.pop()
    else:
        total_ref, peak_ref = refs.pop(), refs.pop()
    if not fresh:
        old_total_ref, old_peak_ref = refs.pop(), refs.pop()
        peak_ref[...] = old_peak_ref[...]
        total_ref[...] = old_total_ref[...]
    if last:
        pieces = refs
        piece_rows = pieces[0].shape[1]

        @pl.when(pl.program_id(0) == 0)
        def _():
            for number, piece in enumerate(pieces):
                for side in range(2):
                    clean[side][pl.ds(number * piece_rows, piece_rows)] = piece[side]

        blocks = [clean]
    else:
        blocks = list(zip(refs[::2], refs[1::2]))
    factor = HD ** (-0.5) * LOG2E
    tile = probs_ref.shape[1]
    ones = jnp.ones((blocks[0][0].shape[0], HD), jnp.bfloat16)
    y, xl, core = scalar_ref[4], scalar_ref[5], scalar_ref[6]
    places = []
    for xl_step in range(NXL):
        for y_step in range(NY):
            y_there = lax.rem(y + y_step, NY)
            xl_there = lax.rem(xl + xl_step, NXL)
            places.append((y_there * NXL + xl_there) * NC + lax.rem(core + pl.program_id(0), NC))

    def one_block(first, k_ref, v_ref):
        def take_scores(head):
            cols = slice(head * HD, (head + 1) * HD)
            rows = jnp.concatenate([q_ref[place, :, cols] for place in places], axis=0)
            scores_ref[head % 2] = lax.dot_general(
                rows, k_ref[:, cols], (((1,), (1,)), ((), ())), preferred_element_type=jnp.float32
            )

        take_scores(0)
        for head in range(HEADS_HERE):
            cols = slice(head * HD, (head + 1) * HD)
            if head + 1 < HEADS_HERE:
                take_scores(head + 1)
            scales = []
            for low in range(0, tile, CHUNK):
                rows = slice(low, low + CHUNK)
                scores = scores_ref[head % 2, rows]
                peak = jnp.max(scores, axis=1, keepdims=True)
                if not first:
                    old_peak = peak_ref[head, rows]
                    peak = jnp.maximum(old_peak, peak)
                    scales.append(jnp.exp2((old_peak - peak) * factor))
                probs_ref[head % 2, rows] = jnp.exp2(((scores - peak) * factor).astype(jnp.bfloat16))
                peak_ref[head, rows] = peak
            wide = jnp.concatenate([v_ref[:, cols], ones], axis=1)
            added = jnp.dot(probs_ref[head % 2], wide, preferred_element_type=jnp.float32)
            total_ref[head] = added if first else total_ref[head] * jnp.concatenate(scales, axis=0) + added

    for number, (k_ref, v_ref) in enumerate(blocks):
        if fresh and number == 0:
            one_block(True, k_ref, v_ref)
        else:
            pl.when(scalar_ref[flags[number]] == 1)(functools.partial(one_block, False, k_ref, v_ref))
    if last:
        for head in range(HEADS_HERE):
            total = total_ref[head]
            out_ref[:, head * HD : (head + 1) * HD] = (total[:, :HD] / total[:, HD:]).astype(jnp.bfloat16)


def attend(scalars, queries, flags, blocks, state=None, last=False):
    rows, width = queries.shape
    fresh = state is None
    share = rows // (NY * NXL * NC)
    tile = rows // NC
    count = len(flags)
    state_specs = [
        pl.BlockSpec((HEADS_HERE, tile, 1), lambda i, *_: (0, i, 0)),
        pl.BlockSpec((HEADS_HERE, tile, 2 * HD), lambda i, *_: (0, i, 0)),
    ]
    in_specs = [pl.BlockSpec((NY * NXL * NC, share, width), lambda i, *_: (0, 0, 0))]
    in_specs += [pl.BlockSpec(block.shape, lambda i, *_, rank=block.ndim: (0,) * rank) for block in blocks]
    operands = [queries.reshape(NY * NXL * NC, share, width), *blocks]
    if not fresh:
        in_specs += state_specs
        operands += state
    scratch = [pltpu.VMEM((2, tile, rows), jnp.bfloat16), pltpu.VMEM((2, tile, rows), jnp.float32)]
    if last:
        out_shape = jax.ShapeDtypeStruct((rows, width), jnp.bfloat16)
        out_specs = pl.BlockSpec((tile, width), lambda i, *_: (i, 0))
        scratch = [
            pltpu.VMEM((HEADS_HERE, tile, 2 * HD), jnp.float32),
            pltpu.VMEM((HEADS_HERE, tile, 1), jnp.float32),
            pltpu.VMEM((rows, width), jnp.bfloat16),
            pltpu.VMEM((rows, width), jnp.bfloat16),
        ] + scratch
    else:
        out_shape = [
            jax.ShapeDtypeStruct((HEADS_HERE, rows, 1), jnp.float32),
            jax.ShapeDtypeStruct((HEADS_HERE, rows, 2 * HD), jnp.float32),
        ]
        out_specs = state_specs
    return pl.pallas_call(
        functools.partial(attend_body, fresh, last, flags),
        out_shape=out_shape,
        grid_spec=pltpu.PrefetchScalarGridSpec(
            num_scalar_prefetch=1, grid=(NC,), in_specs=in_specs, out_specs=out_specs, scratch_shapes=scratch
        ),
        compiler_params=pltpu.CompilerParams(vmem_limit_bytes=40 * 1024 * 1024),
        cost_estimate=pl.CostEstimate(
            flops=4 * count * rows * rows * width, bytes_accessed=20 * rows * width, transcendentals=3 * count * rows * rows
        ),
    )(scalars, *operands)


def fetch(keys, values, root, z, xh, weight, first_pass):
    rows, width = keys.shape
    cut = rows // NZ
    own = jnp.stack([keys.reshape(NZ, cut, width), values.reshape(NZ, cut, width)], axis=1)
    distance = lax.rem(z - root // NXH + NZ, NZ)
    at_root = distance == 0
    up = shift(own[2], "z", NZ, 1)
    keys_late, up = lax.optimization_barrier((keys, up))
    lag2_keys = shift(keys_late, "z", NZ, 1)
    up = shift(jnp.where(at_root, own[1], up), "z", NZ, 1)
    values_late, up = lax.optimization_barrier((values, up))
    lag2_values = shift(values_late, "z", NZ, 1)
    down = shift(own[3], "z", NZ, -1)
    for number in range(4, NZ):
        if number == 5:
            down, _ = lax.optimization_barrier((down, up))
        if number == 6:
            down, lag2_keys = lax.optimization_barrier((down, lag2_keys))
        down = shift(jnp.where(at_root, own[number], down), "z", NZ, -1)
    lag1_keys = lax.ppermute(jnp.where(xh == 0, keys, lag2_keys), "xh", SWAP)
    piece = jnp.where(at_root, own[0], jnp.where(distance <= 2, up, down))
    piece, lag1_keys = lax.optimization_barrier((piece, lag1_keys))
    piece = jnp.where(xh == lax.rem(root, NXH), piece, lax.ppermute(piece, "xh", SWAP))
    piece, lag2_values = lax.optimization_barrier((piece, lag2_values))
    lag1_values = lax.ppermute(jnp.where(xh == 0, values, lag2_values), "xh", SWAP)
    peak, total = first_pass([lag2_keys, lag2_values])
    pieces = [piece]
    up = down = piece
    for number in range(4):
        if number == 1:
            up, peak = lax.optimization_barrier((up, peak))
        if number == 2:
            peak, weight = lax.optimization_barrier((peak, weight))
            up, peak = lax.optimization_barrier((up, peak))
        up = shift(up, "z", NZ, 1)
        pieces.append(up)
        if number < 3:
            down = shift(down, "z", NZ, -1)
            pieces.append(down)
    return [peak, total], [lag1_keys, lag1_values], pieces, weight


def add(*terms):
    total = terms[0].astype(jnp.float32)
    for term in terms[1:]:
        total = total + term.astype(jnp.float32)
    return total


def sum_over_y(terms):
    half = terms[0].shape[-1] // 2
    from_below = shift(terms[2][..., :half], "y", NY, 1)
    from_above = shift(terms[2][..., half:], "y", NY, -1)
    rise = jnp.concatenate([add(terms[1][..., :half], from_below).astype(jnp.bfloat16), terms[1][..., half:]], axis=-1)
    fall = jnp.concatenate([terms[3][..., :half], add(terms[3][..., half:], from_above).astype(jnp.bfloat16)], axis=-1)
    return [terms[0], shift(rise, "y", NY, 1), shift(fall, "y", NY, -1)]


def local(queries, keys, values, residual, out_weight, gate_table, noise_steps, windows):
    z, xh, y, xl, core = (lax.axis_index(name) for name in ("z", "xh", "y", "xl", "c"))
    my_span = z * NXH + xh
    span_ids = lax.iota(jnp.int32, NZ * NXH)
    clean_root = jnp.sum(span_ids * (noise_steps == 0).astype(jnp.int32))
    rows, width = queries.shape
    share = residual.shape[0]

    weight = jnp.concatenate([out_weight, lax.ppermute(out_weight, "c", SWAP)], axis=0)
    scalars = jnp.stack(
        [
            jnp.int32(1),
            windows[my_span, 1],
            windows[my_span, 0],
            (my_span != clean_root).astype(jnp.int32),
            y,
            xl,
            core,
        ]
    )
    def first_pass(lag2):
        return attend(scalars, queries, (0, 1), [keys, values, *lag2])

    state, lag1, pieces, weight = fetch(keys, values, clean_root, z, xh, weight, first_pass)
    state = attend(scalars, queries, (2,), lag1, state)
    attended = attend(scalars, queries, (3,), pieces, state, last=True)
    taken = lax.ppermute(attended[rows // 2 :], "c", SWAP)
    both = jnp.concatenate([attended[: rows // 2], taken], axis=1)

    def project(low, high):
        terms = jnp.dot(both, weight[:, low:high], preferred_element_type=jnp.float32).astype(jnp.bfloat16)
        return terms.reshape(NXL, NY, share, high - low)

    x_first = project(0, X_FIRST)
    y_first = project(X_FIRST, out_weight.shape[1])

    x_got = lax.ppermute(x_first[1], "xl", SWAP)
    here = sum_over_y([y_first[:, number] for number in range(NY)])
    here_kept = [term[0] for term in here]
    here_sent = add(*[term[1] for term in here]).astype(jnp.bfloat16)
    here_got = lax.ppermute(here_sent, "xl", SWAP)
    x_sum = add(x_first[0], x_got).astype(jnp.bfloat16)
    left = add(*sum_over_y([x_sum[number] for number in range(NY)]))
    right = add(*here_kept, here_got)
    gate_row = lax.dynamic_slice_in_dim(gate_table, noise_steps[my_span], 1, 0)
    summed = jnp.concatenate([left, right], axis=1)
    return (residual.astype(jnp.float32) + gate_row * summed).astype(jnp.bfloat16)


def solution(mesh):
    fine = Mesh(mesh.devices.reshape(NZ, NXH, NY, NXL, NC), ("z", "xh", "y", "xl", "c"))
    span, mp = ("z", "xh"), ("y", "xl", "c")
    in_specs = (
        P(span, mp),
        P(span, mp),
        P(span, mp),
        P(span + mp, None),
        P(mp, None),
        P(),
        P(),
        P(),
    )
    out_specs = P(span + mp, None)
    return jax.shard_map(local, mesh=fine, in_specs=in_specs, out_specs=out_specs, check_vma=False)
```

```python
import functools
import math

import jax
import jax.numpy as jnp
from jax import lax
from jax.experimental import pallas as pl
from jax.experimental.pallas import tpu as pltpu
from jax.sharding import Mesh, PartitionSpec as P

HD = 128
HEADS_HERE = 3
NZ, NXH, NY, NXL, NC = 8, 2, 4, 2, 2
X_FIRST = 2560
CHUNK = 16
UP = 2
LOG2E = math.log2(math.e)
SWAP = [(0, 1), (1, 0)]


def shift(value, axis, count, steps):
    return lax.ppermute(value, axis, [(i, (i + steps) % count) for i in range(count)])


def attend_body(fresh, last, flags, *refs):
    refs = list(refs)
    scalar_ref, q_ref = refs.pop(0), refs.pop(0)
    scores_ref, probs_ref = refs.pop(), refs.pop()
    if last:
        clean = (refs.pop(), refs.pop())
        peak_ref, total_ref, out_ref = refs.pop(), refs.pop(), refs.pop()
    else:
        total_ref, peak_ref = refs.pop(), refs.pop()
    if not fresh:
        old_total_ref, old_peak_ref = refs.pop(), refs.pop()
        peak_ref[...] = old_peak_ref[...]
        total_ref[...] = old_total_ref[...]
    if last:
        pieces = refs
        piece_rows = pieces[0].shape[1]

        @pl.when(pl.program_id(0) == 0)
        def _():
            for number, piece in enumerate(pieces):
                for side in range(2):
                    clean[side][pl.ds(number * piece_rows, piece_rows)] = piece[side]

        blocks = [clean]
    else:
        blocks = list(zip(refs[::2], refs[1::2]))
    factor = HD ** (-0.5) * LOG2E
    tile = probs_ref.shape[1]
    ones = jnp.ones((blocks[0][0].shape[0], HD), jnp.bfloat16)
    y, xl, core = scalar_ref[4], scalar_ref[5], scalar_ref[6]
    places = []
    for xl_step in range(NXL):
        for y_step in range(NY):
            y_there = lax.rem(y + y_step, NY)
            xl_there = lax.rem(xl + xl_step, NXL)
            places.append((y_there * NXL + xl_there) * NC + lax.rem(core + pl.program_id(0), NC))

    def one_block(first, k_ref, v_ref):
        def take_scores(head):
            cols = slice(head * HD, (head + 1) * HD)
            rows = jnp.concatenate([q_ref[place, :, cols] for place in places], axis=0)
            scores_ref[head % 2] = lax.dot_general(
                rows, k_ref[:, cols], (((1,), (1,)), ((), ())), preferred_element_type=jnp.float32
            )

        take_scores(0)
        for head in range(HEADS_HERE):
            cols = slice(head * HD, (head + 1) * HD)
            if head + 1 < HEADS_HERE:
                take_scores(head + 1)
            scales = []
            for low in range(0, tile, CHUNK):
                rows = slice(low, low + CHUNK)
                scores = scores_ref[head % 2, rows]
                peak = jnp.max(scores, axis=1, keepdims=True)
                if not first:
                    old_peak = peak_ref[head, rows]
                    peak = jnp.maximum(old_peak, peak)
                    scales.append(jnp.exp2((old_peak - peak) * factor))
                probs_ref[head % 2, rows] = jnp.exp2(((scores - peak) * factor).astype(jnp.bfloat16))
                peak_ref[head, rows] = peak
            wide = jnp.concatenate([v_ref[:, cols], ones], axis=1)
            added = jnp.dot(probs_ref[head % 2], wide, preferred_element_type=jnp.float32)
            total_ref[head] = added if first else total_ref[head] * jnp.concatenate(scales, axis=0) + added

    for number, (k_ref, v_ref) in enumerate(blocks):
        if fresh and number == 0:
            one_block(True, k_ref, v_ref)
        else:
            pl.when(scalar_ref[flags[number]] == 1)(functools.partial(one_block, False, k_ref, v_ref))
    if last:
        for head in range(HEADS_HERE):
            total = total_ref[head]
            out_ref[:, head * HD : (head + 1) * HD] = (total[:, :HD] / total[:, HD:]).astype(jnp.bfloat16)


def attend(scalars, queries, flags, blocks, state=None, last=False):
    rows, width = queries.shape
    fresh = state is None
    share = rows // (NY * NXL * NC)
    tile = rows // NC
    count = len(flags)
    state_specs = [
        pl.BlockSpec((HEADS_HERE, tile, 1), lambda i, *_: (0, i, 0)),
        pl.BlockSpec((HEADS_HERE, tile, 2 * HD), lambda i, *_: (0, i, 0)),
    ]
    in_specs = [pl.BlockSpec((NY * NXL * NC, share, width), lambda i, *_: (0, 0, 0))]
    in_specs += [pl.BlockSpec(block.shape, lambda i, *_, rank=block.ndim: (0,) * rank) for block in blocks]
    operands = [queries.reshape(NY * NXL * NC, share, width), *blocks]
    if not fresh:
        in_specs += state_specs
        operands += state
    scratch = [pltpu.VMEM((2, tile, rows), jnp.bfloat16), pltpu.VMEM((2, tile, rows), jnp.float32)]
    if last:
        out_shape = jax.ShapeDtypeStruct((rows, width), jnp.bfloat16)
        out_specs = pl.BlockSpec((tile, width), lambda i, *_: (i, 0))
        scratch = [
            pltpu.VMEM((HEADS_HERE, tile, 2 * HD), jnp.float32),
            pltpu.VMEM((HEADS_HERE, tile, 1), jnp.float32),
            pltpu.VMEM((rows, width), jnp.bfloat16),
            pltpu.VMEM((rows, width), jnp.bfloat16),
        ] + scratch
    else:
        out_shape = [
            jax.ShapeDtypeStruct((HEADS_HERE, rows, 1), jnp.float32),
            jax.ShapeDtypeStruct((HEADS_HERE, rows, 2 * HD), jnp.float32),
        ]
        out_specs = state_specs
    return pl.pallas_call(
        functools.partial(attend_body, fresh, last, flags),
        out_shape=out_shape,
        grid_spec=pltpu.PrefetchScalarGridSpec(
            num_scalar_prefetch=1, grid=(NC,), in_specs=in_specs, out_specs=out_specs, scratch_shapes=scratch
        ),
        compiler_params=pltpu.CompilerParams(vmem_limit_bytes=40 * 1024 * 1024),
        cost_estimate=pl.CostEstimate(
            flops=4 * count * rows * rows * width, bytes_accessed=20 * rows * width, transcendentals=3 * count * rows * rows
        ),
    )(scalars, *operands)


def fetch(keys, values, root, z, xh, weight, first_pass):
    rows, width = keys.shape
    cut = rows // NZ
    own = jnp.stack([keys.reshape(NZ, cut, width), values.reshape(NZ, cut, width)], axis=1)
    distance = lax.rem(z - root // NXH + NZ, NZ)
    at_root = distance == 0
    lag2_keys = shift(keys, "z", NZ, 1)
    down = shift(own[UP + 1], "z", NZ, -1)
    for number in range(UP + 2, NZ):
        if number == UP + 4:
            down, lag2_keys = lax.optimization_barrier((down, lag2_keys))
        down = shift(jnp.where(at_root, own[number], down), "z", NZ, -1)
    lag1_keys = lax.ppermute(jnp.where(xh == 0, keys, lag2_keys), "xh", SWAP)
    up, lag2_keys = lax.optimization_barrier((own[UP], lag2_keys))
    for number in range(UP, 0, -1):
        up = shift(jnp.where(at_root, own[number], up) if number < UP else up, "z", NZ, 1)
    values_late, up = lax.optimization_barrier((values, up))
    lag2_values = shift(values_late, "z", NZ, 1)
    piece = jnp.where(at_root, own[0], jnp.where(distance <= UP, up, down))
    piece, lag1_keys = lax.optimization_barrier((piece, lag1_keys))
    root, weight = lax.optimization_barrier((root, weight))
    piece = jnp.where(xh == lax.rem(root, NXH), piece, lax.ppermute(piece, "xh", SWAP))
    piece, lag2_values = lax.optimization_barrier((piece, lag2_values))
    lag1_values = lax.ppermute(jnp.where(xh == 0, values, lag2_values), "xh", SWAP)
    peak, total = first_pass([lag2_keys, lag2_values])
    pieces = [piece]
    up = down = piece
    for number in range(4):
        if number == 1:
            up, peak = lax.optimization_barrier((up, peak))
        if number == 2:
            up, lag1_values = lax.optimization_barrier((up, lag1_values))
        up = shift(up, "z", NZ, 1)
        pieces.append(up)
        if number < 3:
            down = shift(down, "z", NZ, -1)
            pieces.append(down)
    return [peak, total], [lag1_keys, lag1_values], pieces, weight


def add(*terms):
    total = terms[0].astype(jnp.float32)
    for term in terms[1:]:
        total = total + term.astype(jnp.float32)
    return total


def sum_over_y(terms):
    half = terms[0].shape[-1] // 2
    from_below = shift(terms[2][..., :half], "y", NY, 1)
    from_above = shift(terms[2][..., half:], "y", NY, -1)
    rise = jnp.concatenate([add(terms[1][..., :half], from_below).astype(jnp.bfloat16), terms[1][..., half:]], axis=-1)
    fall = jnp.concatenate([terms[3][..., :half], add(terms[3][..., half:], from_above).astype(jnp.bfloat16)], axis=-1)
    return [terms[0], shift(rise, "y", NY, 1), shift(fall, "y", NY, -1)]


def local(queries, keys, values, residual, out_weight, gate_table, noise_steps, windows):
    z, xh, y, xl, core = (lax.axis_index(name) for name in ("z", "xh", "y", "xl", "c"))
    my_span = z * NXH + xh
    span_ids = lax.iota(jnp.int32, NZ * NXH)
    clean_root = jnp.sum(span_ids * (noise_steps == 0).astype(jnp.int32))
    rows, width = queries.shape
    share = residual.shape[0]

    weight = jnp.concatenate([out_weight, lax.ppermute(out_weight, "c", SWAP)], axis=0)
    scalars = jnp.stack(
        [
            jnp.int32(1),
            windows[my_span, 1],
            windows[my_span, 0],
            (my_span != clean_root).astype(jnp.int32),
            y,
            xl,
            core,
        ]
    )
    def first_pass(lag2):
        return attend(scalars, queries, (0, 1), [keys, values, *lag2])

    state, lag1, pieces, weight = fetch(keys, values, clean_root, z, xh, weight, first_pass)
    state = attend(scalars, queries, (2,), lag1, state)
    attended = attend(scalars, queries, (3,), pieces, state, last=True)
    taken = lax.ppermute(attended[rows // 2 :], "c", SWAP)
    both = jnp.concatenate([attended[: rows // 2], taken], axis=1)

    def project(low, high):
        terms = jnp.dot(both, weight[:, low:high], preferred_element_type=jnp.float32).astype(jnp.bfloat16)
        return terms.reshape(NXL, NY, share, high - low)

    x_first = project(0, X_FIRST)
    y_first = project(X_FIRST, out_weight.shape[1])

    x_got = lax.ppermute(x_first[1], "xl", SWAP)
    here = sum_over_y([y_first[:, number] for number in range(NY)])
    here_kept = [term[0] for term in here]
    here_sent = add(*[term[1] for term in here]).astype(jnp.bfloat16)
    here_got = lax.ppermute(here_sent, "xl", SWAP)
    x_sum = add(x_first[0], x_got).astype(jnp.bfloat16)
    left = add(*sum_over_y([x_sum[number] for number in range(NY)]))
    right = add(*here_kept, here_got)
    gate_row = lax.dynamic_slice_in_dim(gate_table, noise_steps[my_span], 1, 0)
    summed = jnp.concatenate([left, right], axis=1)
    return (residual.astype(jnp.float32) + gate_row * summed).astype(jnp.bfloat16)


def solution(mesh):
    fine = Mesh(mesh.devices.reshape(NZ, NXH, NY, NXL, NC), ("z", "xh", "y", "xl", "c"))
    span, mp = ("z", "xh"), ("y", "xl", "c")
    in_specs = (
        P(span, mp),
        P(span, mp),
        P(span, mp),
        P(span + mp, None),
        P(mp, None),
        P(),
        P(),
        P(),
    )
    out_specs = P(span + mp, None)
    return jax.shard_map(local, mesh=fine, in_specs=in_specs, out_specs=out_specs, check_vma=False)
```

```python
import functools
import math

import jax
import jax.numpy as jnp
from jax import lax
from jax.experimental import pallas as pl
from jax.experimental.pallas import tpu as pltpu
from jax.sharding import Mesh, PartitionSpec as P

HD = 128
HEADS_HERE = 3
NZ, NXH, NY, NXL, NC = 8, 2, 4, 2, 2
X_FIRST = 2688
CHUNK = 16
UP = 2
OWN, LAG1, LAG2, CLEAN = range(4)
LIVE = 3
LOG2E = math.log2(math.e)
SWAP = [(0, 1), (1, 0)]


def shift(value, axis, count, steps):
    return lax.ppermute(value, axis, [(i, (i + steps) % count) for i in range(count)])


def attend_body(blocks, base, scalar_ref, q_ref, *refs):
    last = blocks[-1] == CLEAN
    refs = list(refs)
    scores_ref, probs_ref = refs.pop(), refs.pop()
    if blocks[0] != OWN:
        v_ref, k_ref = refs.pop(), refs.pop()
    if last:
        out_ref = refs.pop()
    else:
        state_ref = refs.pop()
    if blocks[0] != OWN:
        old_ref = refs.pop()
        pieces = refs if last else [refs[0].at[number] for number in range(NZ)]
        cut = pieces[0].shape[1]

        @pl.when(pl.program_id(0) == 0)
        def _():
            for number, piece in enumerate(pieces):
                k_ref[pl.ds(number * cut, cut)] = piece[0]
                v_ref[pl.ds(number * cut, cut)] = piece[1]

        refs = [k_ref, v_ref]
    factor = HD ** (-0.5) * LOG2E
    group = probs_ref.shape[1]
    ones = jnp.ones((refs[0].shape[0], HD), jnp.bfloat16)
    in_sum = lax.broadcasted_iota(jnp.int32, (group, HD), 1) < HD // 2
    y, xl = scalar_ref[1], scalar_ref[2]
    core = lax.rem(scalar_ref[3] + base + pl.program_id(0), NC)
    places = []
    for xl_step in range(NXL):
        for y_step in range(NY):
            places.append((lax.rem(y + y_step, NY) * NXL + lax.rem(xl + xl_step, NXL)) * NC + core)
    places_each = group // q_ref.shape[1]
    units = [(head, part) for head in range(HEADS_HERE) for part in range(len(places) // places_each)]

    def compute(k_ref, v_ref, from_ref):
        def take_scores(unit):
            head, part = units[unit]
            cols = slice(head * HD, (head + 1) * HD)
            held = places[part * places_each : (part + 1) * places_each]
            rows = jnp.concatenate([q_ref[place, :, cols] for place in held], axis=0)
            scores_ref[unit % 2] = lax.dot_general(
                rows, k_ref[:, cols], (((1,), (1,)), ((), ())), preferred_element_type=jnp.float32
            )

        take_scores(0)
        for unit, (head, part) in enumerate(units):
            cols = slice(head * HD, (head + 1) * HD)
            start = part * group
            if unit + 1 < len(units):
                take_scores(unit + 1)
            scales, peaks = [], []
            for low in range(0, group, CHUNK):
                rows = slice(low, low + CHUNK)
                scores = scores_ref[unit % 2, rows]
                peak = jnp.max(scores, axis=1, keepdims=True)
                if from_ref is not None:
                    old_peak = from_ref[head, start + low : start + low + CHUNK, 2 * HD - 1 :]
                    peak = jnp.maximum(old_peak, peak)
                    scales.append(jnp.exp2((old_peak - peak) * factor))
                probs_ref[unit % 2, rows] = jnp.exp2(((scores - peak) * factor).astype(jnp.bfloat16))
                peaks.append(peak)
            wide = jnp.concatenate([v_ref[:, cols], ones], axis=1)
            added = jnp.dot(probs_ref[unit % 2], wide, preferred_element_type=jnp.float32)
            there = slice(start, start + group)
            if from_ref is not None:
                added = from_ref[head, there] * jnp.concatenate(scales, axis=0) + added
            if last:
                out_ref[there, cols] = (added[:, :HD] / added[:, HD : HD + 1]).astype(jnp.bfloat16)
            else:
                state_ref[head, there, :HD] = added[:, :HD]
                state_ref[head, there, HD:] = jnp.where(in_sum, added[:, HD:], jnp.concatenate(peaks, axis=0))

    for number, block in enumerate(blocks):
        k_ref, v_ref = refs[2 * number : 2 * number + 2]
        if block == OWN:
            compute(k_ref, v_ref, None)
            continue
        live = scalar_ref[LIVE + block] == 1
        from_ref = state_ref if number else old_ref
        pl.when(live)(functools.partial(compute, k_ref, v_ref, from_ref))
        if number == 0:

            @pl.when(jnp.logical_not(live))
            def _():
                if last:
                    for head in range(HEADS_HERE):
                        cols = slice(head * HD, (head + 1) * HD)
                        out_ref[:, cols] = (old_ref[head, :, :HD] / old_ref[head, :, HD : HD + 1]).astype(jnp.bfloat16)
                else:
                    state_ref[...] = old_ref[...]


def attend(blocks, scalars, queries, arrays, state=(), halves=(0, 1)):
    rows, width = queries.shape
    share = rows // (NY * NXL * NC)
    tile = rows // NC
    group = tile // 2
    state_spec = pl.BlockSpec((HEADS_HERE, tile, 2 * HD), lambda i, *_: (0, i + halves[0], 0))
    in_specs = [pl.BlockSpec((NY * NXL * NC, share, width), lambda i, *_: (0, 0, 0))]
    in_specs += [pl.BlockSpec(array.shape, lambda i, *_, rank=array.ndim: (0,) * rank) for array in arrays]
    in_specs += [state_spec] * len(state)
    scratch = [pltpu.VMEM((2, group, rows), jnp.bfloat16), pltpu.VMEM((2, group, rows), jnp.float32)]
    if blocks[0] != OWN:
        scratch = [pltpu.VMEM((rows, width), jnp.bfloat16)] * 2 + scratch
    if blocks[-1] == CLEAN:
        out_shape = jax.ShapeDtypeStruct((tile * len(halves), width), jnp.bfloat16)
        out_specs = pl.BlockSpec((tile, width), lambda i, *_: (i, 0))
    else:
        out_shape = jax.ShapeDtypeStruct((HEADS_HERE, rows, 2 * HD), jnp.float32)
        out_specs = state_spec
    work = len(halves) * len(blocks) * rows * rows
    return pl.pallas_call(
        functools.partial(attend_body, blocks, halves[0]),
        out_shape=out_shape,
        grid_spec=pltpu.PrefetchScalarGridSpec(
            num_scalar_prefetch=1, grid=(len(halves),), in_specs=in_specs, out_specs=out_specs, scratch_shapes=scratch
        ),
        compiler_params=pltpu.CompilerParams(vmem_limit_bytes=40 * 1024 * 1024),
        cost_estimate=pl.CostEstimate(flops=2 * work * width, bytes_accessed=20 * rows * width, transcendentals=2 * work),
    )(scalars, queries.reshape(NY * NXL * NC, share, width), *arrays, *state)


def fetch(keys, values, root, z, xh, state, lag2_pass):
    rows, width = keys.shape
    cut = rows // NZ
    own = jnp.stack([keys.reshape(NZ, cut, width), values.reshape(NZ, cut, width)], axis=1)
    distance = lax.rem(z - root // NXH + NZ, NZ)
    at_root = distance == 0
    up = shift(own[2], "z", NZ, 1)
    down = shift(own[3], "z", NZ, -1)
    up = shift(jnp.where(at_root, own[1], up), "z", NZ, 1)
    own_late, up = lax.optimization_barrier((own, up))
    lag2 = shift(own_late, "z", NZ, 1)
    for number in range(4, NZ):
        if number == 5:
            down, up = lax.optimization_barrier((down, up))
        if number == 6:
            down, state = lax.optimization_barrier((down, state))
        down = shift(jnp.where(at_root, own[number], down), "z", NZ, -1)
    piece = jnp.where(at_root, own[0], jnp.where(distance <= 2, up, down))
    piece = jnp.where(xh == lax.rem(root, NXH), piece, lax.ppermute(piece, "xh", SWAP))
    piece, lag2 = lax.optimization_barrier((piece, lag2))
    lag1 = lax.ppermute(jnp.where(xh == 0, own, lag2), "xh", SWAP)
    state = lag2_pass(lag2, state)
    pieces = [piece]
    up = down = piece
    for number in range(4):
        if number == 1:
            up, state = lax.optimization_barrier((up, state))
        up = shift(up, "z", NZ, 1)
        pieces.append(up)
        if number < 3:
            down = shift(down, "z", NZ, -1)
            pieces.append(down)
    return state, lag1, pieces


def add(*terms):
    total = terms[0].astype(jnp.float32)
    for term in terms[1:]:
        total = total + term.astype(jnp.float32)
    return total


def sum_over_y(terms):
    half = terms[0].shape[-1] // 2
    from_below = shift(terms[2][..., :half], "y", NY, 1)
    from_above = shift(terms[2][..., half:], "y", NY, -1)
    rise = jnp.concatenate([add(terms[1][..., :half], from_below).astype(jnp.bfloat16), terms[1][..., half:]], axis=-1)
    fall = jnp.concatenate([terms[3][..., :half], add(terms[3][..., half:], from_above).astype(jnp.bfloat16)], axis=-1)
    return [terms[0], shift(rise, "y", NY, 1), shift(fall, "y", NY, -1)]


def local(queries, keys, values, residual, out_weight, gate_table, noise_steps, windows):
    z, xh, y, xl, core = (lax.axis_index(name) for name in ("z", "xh", "y", "xl", "c"))
    my_span = z * NXH + xh
    span_ids = lax.iota(jnp.int32, NZ * NXH)
    clean_root = jnp.sum(span_ids * (noise_steps == 0).astype(jnp.int32))
    rows, width = queries.shape
    share = residual.shape[0]

    scalars = jnp.stack(
        [
            jnp.int32(1),
            y,
            xl,
            core,
            windows[my_span, 0],
            windows[my_span, 1],
            (my_span != clean_root).astype(jnp.int32),
        ]
    )
    sibling_weight = lax.ppermute(out_weight, "c", SWAP)
    state = attend((OWN,), scalars, queries, [keys, values])

    def lag2_pass(lag2, state):
        return attend((LAG2,), scalars, queries, [lag2], [state])

    state, lag1, pieces = fetch(keys, values, clean_root, z, xh, state, lag2_pass)
    state = attend((LAG1,), scalars, queries, [lag1], [state])
    attended = attend((CLEAN,), scalars, queries, pieces, [state])
    kept, taken = attended[: rows // 2], lax.ppermute(attended[rows // 2 :], "c", SWAP)

    def project(taken, low, high):
        terms = jnp.dot(kept, out_weight[:, low:high], preferred_element_type=jnp.float32)
        terms = terms + jnp.dot(taken, sibling_weight[:, low:high], preferred_element_type=jnp.float32)
        return terms.astype(jnp.bfloat16).reshape(NXL, NY, share, high - low)

    x_first = project(taken, 0, X_FIRST)
    y_first = project(taken, X_FIRST, out_weight.shape[1])

    x_got = lax.ppermute(x_first[1], "xl", SWAP)
    here = sum_over_y([y_first[:, number] for number in range(NY)])
    here_kept = [term[0] for term in here]
    here_sent = add(*[term[1] for term in here]).astype(jnp.bfloat16)
    here_got = lax.ppermute(here_sent, "xl", SWAP)
    x_sum = add(x_first[0], x_got).astype(jnp.bfloat16)
    left = add(x_sum[0], *[shift(x_sum[step], "y", NY, step) for step in (1, 3, 2)])
    right = add(*here_kept, here_got)
    gate_row = lax.dynamic_slice_in_dim(gate_table, noise_steps[my_span], 1, 0)
    summed = jnp.concatenate([left, right], axis=1)
    return (residual.astype(jnp.float32) + gate_row * summed).astype(jnp.bfloat16)


def solution(mesh):
    fine = Mesh(mesh.devices.reshape(NZ, NXH, NY, NXL, NC), ("z", "xh", "y", "xl", "c"))
    span, mp = ("z", "xh"), ("y", "xl", "c")
    in_specs = (
        P(span, mp),
        P(span, mp),
        P(span, mp),
        P(span + mp, None),
        P(mp, None),
        P(),
        P(),
        P(),
    )
    out_specs = P(span + mp, None)
    return jax.shard_map(local, mesh=fine, in_specs=in_specs, out_specs=out_specs, check_vma=False)
```

```python
import functools
import math

import jax
import jax.numpy as jnp
from jax import lax
from jax.experimental import pallas as pl
from jax.experimental.pallas import tpu as pltpu
from jax.sharding import Mesh, PartitionSpec as P

HD = 128
HEADS_HERE = 3
NZ, NXH, NY, NXL, NC = 8, 2, 4, 2, 2
X_FIRST = 2688
CHUNK = 16
UP = 2
LOG2E = math.log2(math.e)
SWAP = [(0, 1), (1, 0)]


def shift(value, axis, count, steps):
    return lax.ppermute(value, axis, [(i, (i + steps) % count) for i in range(count)])


def attend_body(fresh, last, flags, *refs):
    refs = list(refs)
    scalar_ref, q_ref = refs.pop(0), refs.pop(0)
    scores_ref, probs_ref = refs.pop(), refs.pop()
    if last:
        clean = (refs.pop(), refs.pop())
        peak_ref, total_ref, out_ref = refs.pop(), refs.pop(), refs.pop()
    else:
        total_ref, peak_ref = refs.pop(), refs.pop()
    if not fresh:
        old_total_ref, old_peak_ref = refs.pop(), refs.pop()
        peak_ref[...] = old_peak_ref[...]
        total_ref[...] = old_total_ref[...]
    if last:
        pieces = refs
        piece_rows = pieces[0].shape[1]

        @pl.when(pl.program_id(0) == 0)
        def _():
            for number, piece in enumerate(pieces):
                for side in range(2):
                    clean[side][pl.ds(number * piece_rows, piece_rows)] = piece[side]

        blocks = [clean]
    else:
        blocks = list(zip(refs[::2], refs[1::2]))
    factor = HD ** (-0.5) * LOG2E
    tile = probs_ref.shape[1]
    ones = jnp.ones((blocks[0][0].shape[0], HD), jnp.bfloat16)
    y, xl, core = scalar_ref[4], scalar_ref[5], scalar_ref[6]
    places = []
    for xl_step in range(NXL):
        for y_step in range(NY):
            y_there = lax.rem(y + y_step, NY)
            xl_there = lax.rem(xl + xl_step, NXL)
            places.append((y_there * NXL + xl_there) * NC + lax.rem(core + pl.program_id(0), NC))

    def one_block(first, k_ref, v_ref):
        def take_scores(head):
            cols = slice(head * HD, (head + 1) * HD)
            rows = jnp.concatenate([q_ref[place, :, cols] for place in places], axis=0)
            scores_ref[head % 2] = lax.dot_general(
                rows, k_ref[:, cols], (((1,), (1,)), ((), ())), preferred_element_type=jnp.float32
            )

        take_scores(0)
        for head in range(HEADS_HERE):
            cols = slice(head * HD, (head + 1) * HD)
            if head + 1 < HEADS_HERE:
                take_scores(head + 1)
            scales = []
            for low in range(0, tile, CHUNK):
                rows = slice(low, low + CHUNK)
                scores = scores_ref[head % 2, rows]
                peak = jnp.max(scores, axis=1, keepdims=True)
                if not first:
                    old_peak = peak_ref[head, rows]
                    peak = jnp.maximum(old_peak, peak)
                    scales.append(jnp.exp2((old_peak - peak) * factor))
                probs_ref[head % 2, rows] = jnp.exp2(((scores - peak) * factor).astype(jnp.bfloat16))
                peak_ref[head, rows] = peak
            wide = jnp.concatenate([v_ref[:, cols], ones], axis=1)
            added = jnp.dot(probs_ref[head % 2], wide, preferred_element_type=jnp.float32)
            total_ref[head] = added if first else total_ref[head] * jnp.concatenate(scales, axis=0) + added

    for number, (k_ref, v_ref) in enumerate(blocks):
        if fresh and number == 0:
            one_block(True, k_ref, v_ref)
        else:
            pl.when(scalar_ref[flags[number]] == 1)(functools.partial(one_block, False, k_ref, v_ref))
    if last:
        for head in range(HEADS_HERE):
            total = total_ref[head]
            out_ref[:, head * HD : (head + 1) * HD] = (total[:, :HD] / total[:, HD:]).astype(jnp.bfloat16)


def attend(scalars, queries, flags, blocks, state=None, last=False):
    rows, width = queries.shape
    fresh = state is None
    share = rows // (NY * NXL * NC)
    tile = rows // NC
    count = len(flags)
    state_specs = [
        pl.BlockSpec((HEADS_HERE, tile, 1), lambda i, *_: (0, i, 0)),
        pl.BlockSpec((HEADS_HERE, tile, 2 * HD), lambda i, *_: (0, i, 0)),
    ]
    in_specs = [pl.BlockSpec((NY * NXL * NC, share, width), lambda i, *_: (0, 0, 0))]
    in_specs += [pl.BlockSpec(block.shape, lambda i, *_, rank=block.ndim: (0,) * rank) for block in blocks]
    operands = [queries.reshape(NY * NXL * NC, share, width), *blocks]
    if not fresh:
        in_specs += state_specs
        operands += state
    scratch = [pltpu.VMEM((2, tile, rows), jnp.bfloat16), pltpu.VMEM((2, tile, rows), jnp.float32)]
    if last:
        out_shape = jax.ShapeDtypeStruct((rows, width), jnp.bfloat16)
        out_specs = pl.BlockSpec((tile, width), lambda i, *_: (i, 0))
        scratch = [
            pltpu.VMEM((HEADS_HERE, tile, 2 * HD), jnp.float32),
            pltpu.VMEM((HEADS_HERE, tile, 1), jnp.float32),
            pltpu.VMEM((rows, width), jnp.bfloat16),
            pltpu.VMEM((rows, width), jnp.bfloat16),
        ] + scratch
    else:
        out_shape = [
            jax.ShapeDtypeStruct((HEADS_HERE, rows, 1), jnp.float32),
            jax.ShapeDtypeStruct((HEADS_HERE, rows, 2 * HD), jnp.float32),
        ]
        out_specs = state_specs
    return pl.pallas_call(
        functools.partial(attend_body, fresh, last, flags),
        out_shape=out_shape,
        grid_spec=pltpu.PrefetchScalarGridSpec(
            num_scalar_prefetch=1, grid=(NC,), in_specs=in_specs, out_specs=out_specs, scratch_shapes=scratch
        ),
        compiler_params=pltpu.CompilerParams(vmem_limit_bytes=40 * 1024 * 1024),
        cost_estimate=pl.CostEstimate(
            flops=4 * count * rows * rows * width, bytes_accessed=20 * rows * width, transcendentals=3 * count * rows * rows
        ),
    )(scalars, *operands)


def fetch(keys, values, root, z, xh, scalars, first_pass):
    rows, width = keys.shape
    cut = rows // NZ
    own = jnp.stack([keys.reshape(NZ, cut, width), values.reshape(NZ, cut, width)], axis=1)
    distance = lax.rem(z - root // NXH + NZ, NZ)
    at_root = distance == 0
    lag2_keys = shift(keys, "z", NZ, 1)
    down = shift(own[UP + 1], "z", NZ, -1)
    for number in range(UP + 2, NZ):
        if number == UP + 3:
            down, scalars = lax.optimization_barrier((down, scalars))
        if number == UP + 4:
            down, lag2_keys = lax.optimization_barrier((down, lag2_keys))
        down = shift(jnp.where(at_root, own[number], down), "z", NZ, -1)
    lag1_keys = lax.ppermute(jnp.where(xh == 0, keys, lag2_keys), "xh", SWAP)
    up, lag2_keys = lax.optimization_barrier((own[UP], lag2_keys))
    for number in range(UP, 0, -1):
        up = shift(jnp.where(at_root, own[number], up) if number < UP else up, "z", NZ, 1)
    values_late, up = lax.optimization_barrier((values, up))
    lag2_values = shift(values_late, "z", NZ, 1)
    piece = jnp.where(at_root, own[0], jnp.where(distance <= UP, up, down))
    piece, lag1_keys = lax.optimization_barrier((piece, lag1_keys))
    piece = jnp.where(xh == lax.rem(root, NXH), piece, lax.ppermute(piece, "xh", SWAP))
    piece, lag2_values = lax.optimization_barrier((piece, lag2_values))
    lag1_values = lax.ppermute(jnp.where(xh == 0, values, lag2_values), "xh", SWAP)
    peak, total = first_pass(scalars, [lag2_keys, lag2_values])
    pieces = [piece]
    up = down = piece
    for number in range(4):
        if number == 1:
            up, peak = lax.optimization_barrier((up, peak))
        if number == 2:
            up, lag1_values = lax.optimization_barrier((up, lag1_values))
        up = shift(up, "z", NZ, 1)
        pieces.append(up)
        if number < 3:
            down = shift(down, "z", NZ, -1)
            pieces.append(down)
    return [peak, total], [lag1_keys, lag1_values], pieces, scalars


def add(*terms):
    total = terms[0].astype(jnp.float32)
    for term in terms[1:]:
        total = total + term.astype(jnp.float32)
    return total


def sum_over_y(terms):
    half = terms[0].shape[-1] // 2
    from_below = shift(terms[2][..., :half], "y", NY, 1)
    from_above = shift(terms[2][..., half:], "y", NY, -1)
    rise = jnp.concatenate([add(terms[1][..., :half], from_below).astype(jnp.bfloat16), terms[1][..., half:]], axis=-1)
    fall = jnp.concatenate([terms[3][..., :half], add(terms[3][..., half:], from_above).astype(jnp.bfloat16)], axis=-1)
    return [terms[0], shift(rise, "y", NY, 1), shift(fall, "y", NY, -1)]


def local(queries, keys, values, residual, out_weight, gate_table, noise_steps, windows):
    z, xh, y, xl, core = (lax.axis_index(name) for name in ("z", "xh", "y", "xl", "c"))
    my_span = z * NXH + xh
    span_ids = lax.iota(jnp.int32, NZ * NXH)
    clean_root = jnp.sum(span_ids * (noise_steps == 0).astype(jnp.int32))
    rows, width = queries.shape
    share = residual.shape[0]

    weight = jnp.concatenate([out_weight, lax.ppermute(out_weight, "c", SWAP)], axis=0)
    scalars = jnp.stack(
        [
            jnp.int32(1),
            windows[my_span, 1],
            windows[my_span, 0],
            (my_span != clean_root).astype(jnp.int32),
            y,
            xl,
            core,
        ]
    )

    def first_pass(scalars, lag2):
        return attend(scalars, queries, (0, 1), [keys, values, *lag2])

    state, lag1, pieces, scalars = fetch(keys, values, clean_root, z, xh, scalars, first_pass)
    state = attend(scalars, queries, (2,), lag1, state)
    state, weight = lax.optimization_barrier((state, weight))
    attended = attend(scalars, queries, (3,), pieces, state, last=True)
    taken = lax.ppermute(attended[rows // 2 :], "c", SWAP)
    both = jnp.concatenate([attended[: rows // 2], taken], axis=1)

    def project(low, high):
        terms = jnp.dot(both, weight[:, low:high], preferred_element_type=jnp.float32).astype(jnp.bfloat16)
        return terms.reshape(NXL, NY, share, high - low)

    x_first = project(0, X_FIRST)
    y_first = project(X_FIRST, out_weight.shape[1])

    x_got = lax.ppermute(x_first[1], "xl", SWAP)
    here = sum_over_y([y_first[:, number] for number in range(NY)])
    here_kept = [term[0] for term in here]
    here_sent = add(*[term[1] for term in here]).astype(jnp.bfloat16)
    here_got = lax.ppermute(here_sent, "xl", SWAP)
    x_sum = add(x_first[0], x_got).astype(jnp.bfloat16)
    left = add(x_sum[0], *[shift(x_sum[step], "y", NY, step) for step in (1, 3, 2)])
    right = add(*here_kept, here_got)
    gate_row = lax.dynamic_slice_in_dim(gate_table, noise_steps[my_span], 1, 0)
    summed = jnp.concatenate([left, right], axis=1)
    return (residual.astype(jnp.float32) + gate_row * summed).astype(jnp.bfloat16)


def solution(mesh):
    fine = Mesh(mesh.devices.reshape(NZ, NXH, NY, NXL, NC), ("z", "xh", "y", "xl", "c"))
    span, mp = ("z", "xh"), ("y", "xl", "c")
    in_specs = (
        P(span, mp),
        P(span, mp),
        P(span, mp),
        P(span + mp, None),
        P(mp, None),
        P(),
        P(),
        P(),
    )
    out_specs = P(span + mp, None)
    return jax.shard_map(local, mesh=fine, in_specs=in_specs, out_specs=out_specs, check_vma=False)
```

```python
import functools
import math

import jax
import jax.numpy as jnp
from jax import lax
from jax.experimental import pallas as pl
from jax.experimental.pallas import tpu as pltpu
from jax.sharding import Mesh, PartitionSpec as P

HD = 128
HEADS_HERE = 3
NZ, NXH, NY, NXL, NC = 8, 2, 4, 2, 2
X_FIRST = 2688
CHUNK = 16
UP = 2
LOG2E = math.log2(math.e)
SWAP = [(0, 1), (1, 0)]


def shift(value, axis, count, steps):
    return lax.ppermute(value, axis, [(i, (i + steps) % count) for i in range(count)])


def attend_body(fresh, last, flags, *refs):
    refs = list(refs)
    scalar_ref, q_ref = refs.pop(0), refs.pop(0)
    scores_ref, probs_ref = refs.pop(), refs.pop()
    if last:
        clean = (refs.pop(), refs.pop())
        peak_ref, total_ref, out_ref = refs.pop(), refs.pop(), refs.pop()
    else:
        total_ref, peak_ref = refs.pop(), refs.pop()
    if not fresh:
        old_total_ref, old_peak_ref = refs.pop(), refs.pop()
        peak_ref[...] = old_peak_ref[...]
        total_ref[...] = old_total_ref[...]
    if last:
        pieces = refs
        piece_rows = pieces[0].shape[1]

        @pl.when(pl.program_id(0) == 0)
        def _():
            for number, piece in enumerate(pieces):
                for side in range(2):
                    clean[side][pl.ds(number * piece_rows, piece_rows)] = piece[side]

        blocks = [clean]
    else:
        blocks = list(zip(refs[::2], refs[1::2]))
    factor = HD ** (-0.5) * LOG2E
    tile = probs_ref.shape[1]
    ones = jnp.ones((blocks[0][0].shape[0], HD), jnp.bfloat16)
    y, xl, core = scalar_ref[4], scalar_ref[5], scalar_ref[6]
    places = []
    for xl_step in range(NXL):
        for y_step in range(NY):
            y_there = lax.rem(y + y_step, NY)
            xl_there = lax.rem(xl + xl_step, NXL)
            places.append((y_there * NXL + xl_there) * NC + lax.rem(core + pl.program_id(0), NC))

    def one_block(first, k_ref, v_ref):
        def take_scores(head):
            cols = slice(head * HD, (head + 1) * HD)
            rows = jnp.concatenate([q_ref[place, :, cols] for place in places], axis=0)
            scores_ref[head % 2] = lax.dot_general(
                rows, k_ref[:, cols], (((1,), (1,)), ((), ())), preferred_element_type=jnp.float32
            )

        take_scores(0)
        for head in range(HEADS_HERE):
            cols = slice(head * HD, (head + 1) * HD)
            if head + 1 < HEADS_HERE:
                take_scores(head + 1)
            scales = []
            for low in range(0, tile, CHUNK):
                rows = slice(low, low + CHUNK)
                scores = scores_ref[head % 2, rows]
                peak = jnp.max(scores, axis=1, keepdims=True)
                if not first:
                    old_peak = peak_ref[head, rows]
                    peak = jnp.maximum(old_peak, peak)
                    scales.append(jnp.exp2((old_peak - peak) * factor))
                probs_ref[head % 2, rows] = jnp.exp2(((scores - peak) * factor).astype(jnp.bfloat16))
                peak_ref[head, rows] = peak
            wide = jnp.concatenate([v_ref[:, cols], ones], axis=1)
            added = jnp.dot(probs_ref[head % 2], wide, preferred_element_type=jnp.float32)
            total_ref[head] = added if first else total_ref[head] * jnp.concatenate(scales, axis=0) + added

    for number, (k_ref, v_ref) in enumerate(blocks):
        if fresh and number == 0:
            one_block(True, k_ref, v_ref)
        else:
            pl.when(scalar_ref[flags[number]] == 1)(functools.partial(one_block, False, k_ref, v_ref))
    if last:
        for head in range(HEADS_HERE):
            total = total_ref[head]
            out_ref[:, head * HD : (head + 1) * HD] = (total[:, :HD] / total[:, HD:]).astype(jnp.bfloat16)


def attend(scalars, queries, flags, blocks, state=None, last=False):
    rows, width = queries.shape
    fresh = state is None
    share = rows // (NY * NXL * NC)
    tile = rows // NC
    count = len(flags)
    state_specs = [
        pl.BlockSpec((HEADS_HERE, tile, 1), lambda i, *_: (0, i, 0)),
        pl.BlockSpec((HEADS_HERE, tile, 2 * HD), lambda i, *_: (0, i, 0)),
    ]
    in_specs = [pl.BlockSpec((NY * NXL * NC, share, width), lambda i, *_: (0, 0, 0))]
    in_specs += [pl.BlockSpec(block.shape, lambda i, *_, rank=block.ndim: (0,) * rank) for block in blocks]
    operands = [queries.reshape(NY * NXL * NC, share, width), *blocks]
    if not fresh:
        in_specs += state_specs
        operands += state
    scratch = [pltpu.VMEM((2, tile, rows), jnp.bfloat16), pltpu.VMEM((2, tile, rows), jnp.float32)]
    if last:
        out_shape = jax.ShapeDtypeStruct((rows, width), jnp.bfloat16)
        out_specs = pl.BlockSpec((tile, width), lambda i, *_: (i, 0))
        scratch = [
            pltpu.VMEM((HEADS_HERE, tile, 2 * HD), jnp.float32),
            pltpu.VMEM((HEADS_HERE, tile, 1), jnp.float32),
            pltpu.VMEM((rows, width), jnp.bfloat16),
            pltpu.VMEM((rows, width), jnp.bfloat16),
        ] + scratch
    else:
        out_shape = [
            jax.ShapeDtypeStruct((HEADS_HERE, rows, 1), jnp.float32),
            jax.ShapeDtypeStruct((HEADS_HERE, rows, 2 * HD), jnp.float32),
        ]
        out_specs = state_specs
    return pl.pallas_call(
        functools.partial(attend_body, fresh, last, flags),
        out_shape=out_shape,
        grid_spec=pltpu.PrefetchScalarGridSpec(
            num_scalar_prefetch=1, grid=(NC,), in_specs=in_specs, out_specs=out_specs, scratch_shapes=scratch
        ),
        compiler_params=pltpu.CompilerParams(vmem_limit_bytes=20 * 1024 * 1024),
        cost_estimate=pl.CostEstimate(
            flops=4 * count * rows * rows * width, bytes_accessed=20 * rows * width, transcendentals=3 * count * rows * rows
        ),
    )(scalars, *operands)


def fetch(keys, values, root, z, xh, scalars, first_pass):
    rows, width = keys.shape
    cut = rows // NZ
    own = jnp.stack([keys.reshape(NZ, cut, width), values.reshape(NZ, cut, width)], axis=1)
    distance = lax.rem(z - root // NXH + NZ, NZ)
    at_root = distance == 0
    lag2_keys = shift(keys, "z", NZ, 1)
    down = shift(own[UP + 1], "z", NZ, -1)
    for number in range(UP + 2, NZ):
        if number == UP + 3:
            down, scalars = lax.optimization_barrier((down, scalars))
        if number == UP + 4:
            down, lag2_keys = lax.optimization_barrier((down, lag2_keys))
        down = shift(jnp.where(at_root, own[number], down), "z", NZ, -1)
    lag1_keys = lax.ppermute(jnp.where(xh == 0, keys, lag2_keys), "xh", SWAP)
    up, lag2_keys = lax.optimization_barrier((own[UP], lag2_keys))
    for number in range(UP, 0, -1):
        up = shift(jnp.where(at_root, own[number], up) if number < UP else up, "z", NZ, 1)
    values_late, up = lax.optimization_barrier((values, up))
    lag2_values = shift(values_late, "z", NZ, 1)
    piece = jnp.where(at_root, own[0], jnp.where(distance <= UP, up, down))
    piece, lag1_keys = lax.optimization_barrier((piece, lag1_keys))
    piece = jnp.where(xh == lax.rem(root, NXH), piece, lax.ppermute(piece, "xh", SWAP))
    piece, lag2_values = lax.optimization_barrier((piece, lag2_values))
    lag1_values = lax.ppermute(jnp.where(xh == 0, values, lag2_values), "xh", SWAP)
    peak, total = first_pass(scalars, [lag2_keys, lag2_values])
    pieces = [piece]
    up = down = piece
    for number in range(4):
        if number == 1:
            up, peak = lax.optimization_barrier((up, peak))
        if number == 2:
            up, lag1_values = lax.optimization_barrier((up, lag1_values))
        up = shift(up, "z", NZ, 1)
        pieces.append(up)
        if number < 3:
            down = shift(down, "z", NZ, -1)
            pieces.append(down)
    return [peak, total], [lag1_keys, lag1_values], pieces, scalars


def add(*terms):
    total = terms[0].astype(jnp.float32)
    for term in terms[1:]:
        total = total + term.astype(jnp.float32)
    return total


def sum_over_y(terms):
    half = terms[0].shape[-1] // 2
    from_below = shift(terms[2][..., :half], "y", NY, 1)
    from_above = shift(terms[2][..., half:], "y", NY, -1)
    rise = jnp.concatenate([add(terms[1][..., :half], from_below).astype(jnp.bfloat16), terms[1][..., half:]], axis=-1)
    fall = jnp.concatenate([terms[3][..., :half], add(terms[3][..., half:], from_above).astype(jnp.bfloat16)], axis=-1)
    return [terms[0], shift(rise, "y", NY, 1), shift(fall, "y", NY, -1)]


def local(queries, keys, values, residual, out_weight, gate_table, noise_steps, windows):
    z, xh, y, xl, core = (lax.axis_index(name) for name in ("z", "xh", "y", "xl", "c"))
    my_span = z * NXH + xh
    span_ids = lax.iota(jnp.int32, NZ * NXH)
    clean_root = jnp.sum(span_ids * (noise_steps == 0).astype(jnp.int32))
    rows, width = queries.shape
    share = residual.shape[0]

    weight = jnp.concatenate([out_weight, lax.ppermute(out_weight, "c", SWAP)], axis=0)
    scalars = jnp.stack(
        [
            jnp.int32(1),
            windows[my_span, 1],
            windows[my_span, 0],
            (my_span != clean_root).astype(jnp.int32),
            y,
            xl,
            core,
        ]
    )

    def first_pass(scalars, lag2):
        return attend(scalars, queries, (0, 1), [keys, values, *lag2])

    state, lag1, pieces, scalars = fetch(keys, values, clean_root, z, xh, scalars, first_pass)
    state = attend(scalars, queries, (2,), lag1, state)
    state, weight = lax.optimization_barrier((state, weight))
    attended = attend(scalars, queries, (3,), pieces, state, last=True)
    taken = lax.ppermute(attended[rows // 2 :], "c", SWAP)
    both = jnp.concatenate([attended[: rows // 2], taken], axis=1)

    def project(low, high):
        terms = jnp.dot(both, weight[:, low:high], preferred_element_type=jnp.float32).astype(jnp.bfloat16)
        return terms.reshape(NXL, NY, share, high - low)

    x_first = project(0, X_FIRST)
    y_first = project(X_FIRST, out_weight.shape[1])

    x_got = lax.ppermute(x_first[1], "xl", SWAP)
    here = sum_over_y([y_first[:, number] for number in range(NY)])
    here_kept = [term[0] for term in here]
    here_sent = add(*[term[1] for term in here]).astype(jnp.bfloat16)
    here_got = lax.ppermute(here_sent, "xl", SWAP)
    x_sum = add(x_first[0], x_got).astype(jnp.bfloat16)
    left = add(x_sum[0], *[shift(x_sum[step], "y", NY, step) for step in (1, 3, 2)])
    right = add(*here_kept, here_got)
    gate_row = lax.dynamic_slice_in_dim(gate_table, noise_steps[my_span], 1, 0)
    summed = jnp.concatenate([left, right], axis=1)
    return (residual.astype(jnp.float32) + gate_row * summed).astype(jnp.bfloat16)


def solution(mesh):
    fine = Mesh(mesh.devices.reshape(NZ, NXH, NY, NXL, NC), ("z", "xh", "y", "xl", "c"))
    span, mp = ("z", "xh"), ("y", "xl", "c")
    in_specs = (
        P(span, mp),
        P(span, mp),
        P(span, mp),
        P(span + mp, None),
        P(mp, None),
        P(),
        P(),
        P(),
    )
    out_specs = P(span + mp, None)
    return jax.shard_map(local, mesh=fine, in_specs=in_specs, out_specs=out_specs, check_vma=False)
```

```python
import functools
import math

import jax
import jax.numpy as jnp
from jax import lax
from jax.experimental import pallas as pl
from jax.experimental.pallas import tpu as pltpu
from jax.sharding import Mesh, PartitionSpec as P

HD = 128
HEADS_HERE = 3
NZ, NXH, NY, NXL, NC = 8, 2, 4, 2, 2
X_FIRST = 2688
CHUNK = 16
UP = 2
LOG2E = math.log2(math.e)
SWAP = [(0, 1), (1, 0)]


def shift(value, axis, count, steps):
    return lax.ppermute(value, axis, [(i, (i + steps) % count) for i in range(count)])


def attend_body(fresh, last, flags, *refs):
    refs = list(refs)
    scalar_ref, q_ref = refs.pop(0), refs.pop(0)
    scores_ref, probs_ref = refs.pop(), refs.pop()
    if last:
        clean = (refs.pop(), refs.pop())
        peak_ref, total_ref, out_ref = refs.pop(), refs.pop(), refs.pop()
    else:
        total_ref, peak_ref = refs.pop(), refs.pop()
    if not fresh:
        old_total_ref, old_peak_ref = refs.pop(), refs.pop()
        peak_ref[...] = old_peak_ref[...]
        total_ref[...] = old_total_ref[...]
    if last:
        pieces = refs
        piece_rows = pieces[0].shape[1]

        @pl.when(pl.program_id(0) == 0)
        def _():
            for number, piece in enumerate(pieces):
                for side in range(2):
                    clean[side][pl.ds(number * piece_rows, piece_rows)] = piece[side]

        blocks = [clean]
    else:
        if len(refs) == 1:
            refs = [refs[0].at[0], refs[0].at[1]]
        blocks = list(zip(refs[::2], refs[1::2]))
    factor = HD ** (-0.5) * LOG2E
    tile = probs_ref.shape[1]
    ones = jnp.ones((blocks[0][0].shape[0], HD), jnp.bfloat16)
    y, xl, core = scalar_ref[4], scalar_ref[5], scalar_ref[6]
    places = []
    for xl_step in range(NXL):
        for y_step in range(NY):
            y_there = lax.rem(y + y_step, NY)
            xl_there = lax.rem(xl + xl_step, NXL)
            places.append((y_there * NXL + xl_there) * NC + lax.rem(core + pl.program_id(0), NC))

    def one_block(first, k_ref, v_ref):
        def take_scores(head):
            cols = slice(head * HD, (head + 1) * HD)
            rows = jnp.concatenate([q_ref[place, :, cols] for place in places], axis=0)
            scores_ref[head % 2] = lax.dot_general(
                rows, k_ref[:, cols], (((1,), (1,)), ((), ())), preferred_element_type=jnp.float32
            )

        take_scores(0)
        for head in range(HEADS_HERE):
            cols = slice(head * HD, (head + 1) * HD)
            if head + 1 < HEADS_HERE:
                take_scores(head + 1)
            scales = []
            for low in range(0, tile, CHUNK):
                rows = slice(low, low + CHUNK)
                scores = scores_ref[head % 2, rows]
                peak = jnp.max(scores, axis=1, keepdims=True)
                if not first:
                    old_peak = peak_ref[head, rows]
                    peak = jnp.maximum(old_peak, peak)
                    scales.append(jnp.exp2((old_peak - peak) * factor))
                probs_ref[head % 2, rows] = jnp.exp2(((scores - peak) * factor).astype(jnp.bfloat16))
                peak_ref[head, rows] = peak
            wide = jnp.concatenate([v_ref[:, cols], ones], axis=1)
            added = jnp.dot(probs_ref[head % 2], wide, preferred_element_type=jnp.float32)
            total_ref[head] = added if first else total_ref[head] * jnp.concatenate(scales, axis=0) + added

    for number, (k_ref, v_ref) in enumerate(blocks):
        if fresh and number == 0:
            one_block(True, k_ref, v_ref)
        else:
            pl.when(scalar_ref[flags[number]] == 1)(functools.partial(one_block, False, k_ref, v_ref))
    if last:
        for head in range(HEADS_HERE):
            total = total_ref[head]
            out_ref[:, head * HD : (head + 1) * HD] = (total[:, :HD] / total[:, HD:]).astype(jnp.bfloat16)


def attend(scalars, queries, flags, blocks, state=None, last=False):
    rows, width = queries.shape
    fresh = state is None
    share = rows // (NY * NXL * NC)
    tile = rows // NC
    count = len(flags)
    state_specs = [
        pl.BlockSpec((HEADS_HERE, tile, 1), lambda i, *_: (0, i, 0)),
        pl.BlockSpec((HEADS_HERE, tile, 2 * HD), lambda i, *_: (0, i, 0)),
    ]
    in_specs = [pl.BlockSpec((NY * NXL * NC, share, width), lambda i, *_: (0, 0, 0))]
    in_specs += [pl.BlockSpec(block.shape, lambda i, *_, rank=block.ndim: (0,) * rank) for block in blocks]
    operands = [queries.reshape(NY * NXL * NC, share, width), *blocks]
    if not fresh:
        in_specs += state_specs
        operands += state
    scratch = [pltpu.VMEM((2, tile, rows), jnp.bfloat16), pltpu.VMEM((2, tile, rows), jnp.float32)]
    if last:
        out_shape = jax.ShapeDtypeStruct((rows, width), jnp.bfloat16)
        out_specs = pl.BlockSpec((tile, width), lambda i, *_: (i, 0))
        scratch = [
            pltpu.VMEM((HEADS_HERE, tile, 2 * HD), jnp.float32),
            pltpu.VMEM((HEADS_HERE, tile, 1), jnp.float32),
            pltpu.VMEM((rows, width), jnp.bfloat16),
            pltpu.VMEM((rows, width), jnp.bfloat16),
        ] + scratch
    else:
        out_shape = [
            jax.ShapeDtypeStruct((HEADS_HERE, rows, 1), jnp.float32),
            jax.ShapeDtypeStruct((HEADS_HERE, rows, 2 * HD), jnp.float32),
        ]
        out_specs = state_specs
    return pl.pallas_call(
        functools.partial(attend_body, fresh, last, flags),
        out_shape=out_shape,
        grid_spec=pltpu.PrefetchScalarGridSpec(
            num_scalar_prefetch=1, grid=(NC,), in_specs=in_specs, out_specs=out_specs, scratch_shapes=scratch
        ),
        compiler_params=pltpu.CompilerParams(vmem_limit_bytes=40 * 1024 * 1024),
        cost_estimate=pl.CostEstimate(
            flops=4 * count * rows * rows * width, bytes_accessed=20 * rows * width, transcendentals=3 * count * rows * rows
        ),
    )(scalars, *operands)


def fetch(keys, values, root, z, xh, scalars, first_pass):
    rows, width = keys.shape
    cut = rows // NZ
    own = jnp.stack([keys.reshape(NZ, cut, width), values.reshape(NZ, cut, width)], axis=1)
    distance = lax.rem(z - root // NXH + NZ, NZ)
    at_root = distance == 0
    lag2_keys = shift(keys, "z", NZ, 1)
    down = shift(own[UP + 1], "z", NZ, -1)
    for number in range(UP + 2, NZ):
        if number == UP + 3:
            down, scalars = lax.optimization_barrier((down, scalars))
        if number == UP + 4:
            down, lag2_keys = lax.optimization_barrier((down, lag2_keys))
        down = shift(jnp.where(at_root, own[number], down), "z", NZ, -1)
    up, lag2_keys = lax.optimization_barrier((own[UP], lag2_keys))
    for number in range(UP, 0, -1):
        up = shift(jnp.where(at_root, own[number], up) if number < UP else up, "z", NZ, 1)
    values_late, up = lax.optimization_barrier((values, up))
    lag2_values = shift(values_late, "z", NZ, 1)
    piece = jnp.where(at_root, own[0], jnp.where(distance <= UP, up, down))
    piece = jnp.where(xh == lax.rem(root, NXH), piece, lax.ppermute(piece, "xh", SWAP))
    piece, lag2_values = lax.optimization_barrier((piece, lag2_values))
    lag1 = jnp.where(xh == 0, jnp.stack([keys, values]), jnp.stack([lag2_keys, lag2_values]))
    lag1 = lax.ppermute(lag1, "xh", SWAP)
    peak, total = first_pass(scalars, [lag2_keys, lag2_values])
    pieces = [piece]
    up = down = piece
    for number in range(4):
        if number == 1:
            up, peak = lax.optimization_barrier((up, peak))
        up = shift(up, "z", NZ, 1)
        pieces.append(up)
        if number < 3:
            down = shift(down, "z", NZ, -1)
            pieces.append(down)
    return [peak, total], lag1, pieces, scalars


def add(*terms):
    total = terms[0].astype(jnp.float32)
    for term in terms[1:]:
        total = total + term.astype(jnp.float32)
    return total


def sum_over_y(terms):
    half = terms[0].shape[-1] // 2
    from_below = shift(terms[2][..., :half], "y", NY, 1)
    from_above = shift(terms[2][..., half:], "y", NY, -1)
    rise = jnp.concatenate([add(terms[1][..., :half], from_below).astype(jnp.bfloat16), terms[1][..., half:]], axis=-1)
    fall = jnp.concatenate([terms[3][..., :half], add(terms[3][..., half:], from_above).astype(jnp.bfloat16)], axis=-1)
    return [terms[0], shift(rise, "y", NY, 1), shift(fall, "y", NY, -1)]


def local(queries, keys, values, residual, out_weight, gate_table, noise_steps, windows):
    z, xh, y, xl, core = (lax.axis_index(name) for name in ("z", "xh", "y", "xl", "c"))
    my_span = z * NXH + xh
    span_ids = lax.iota(jnp.int32, NZ * NXH)
    clean_root = jnp.sum(span_ids * (noise_steps == 0).astype(jnp.int32))
    rows, width = queries.shape
    share = residual.shape[0]

    weight = jnp.concatenate([out_weight, lax.ppermute(out_weight, "c", SWAP)], axis=0)
    scalars = jnp.stack(
        [
            jnp.int32(1),
            windows[my_span, 1],
            windows[my_span, 0],
            (my_span != clean_root).astype(jnp.int32),
            y,
            xl,
            core,
        ]
    )

    def first_pass(scalars, lag2):
        return attend(scalars, queries, (0, 1), [keys, values, *lag2])

    state, lag1, pieces, scalars = fetch(keys, values, clean_root, z, xh, scalars, first_pass)
    state, weight = lax.optimization_barrier((state, weight))
    state = attend(scalars, queries, (2,), [lag1], state)
    attended = attend(scalars, queries, (3,), pieces, state, last=True)
    taken = lax.ppermute(attended[rows // 2 :], "c", SWAP)
    both = jnp.concatenate([attended[: rows // 2], taken], axis=1)

    def project(low, high):
        terms = jnp.dot(both, weight[:, low:high], preferred_element_type=jnp.float32).astype(jnp.bfloat16)
        return terms.reshape(NXL, NY, share, high - low)

    x_first = project(0, X_FIRST)
    y_first = project(X_FIRST, out_weight.shape[1])

    x_got = lax.ppermute(x_first[1], "xl", SWAP)
    here = sum_over_y([y_first[:, number] for number in range(NY)])
    here_kept = [term[0] for term in here]
    here_sent = add(*[term[1] for term in here]).astype(jnp.bfloat16)
    here_got = lax.ppermute(here_sent, "xl", SWAP)
    x_sum = add(x_first[0], x_got).astype(jnp.bfloat16)
    left = add(x_sum[0], *[shift(x_sum[step], "y", NY, step) for step in (1, 3, 2)])
    right = add(*here_kept, here_got)
    gate_row = lax.dynamic_slice_in_dim(gate_table, noise_steps[my_span], 1, 0)
    summed = jnp.concatenate([left, right], axis=1)
    return (residual.astype(jnp.float32) + gate_row * summed).astype(jnp.bfloat16)


def solution(mesh):
    fine = Mesh(mesh.devices.reshape(NZ, NXH, NY, NXL, NC), ("z", "xh", "y", "xl", "c"))
    span, mp = ("z", "xh"), ("y", "xl", "c")
    in_specs = (
        P(span, mp),
        P(span, mp),
        P(span, mp),
        P(span + mp, None),
        P(mp, None),
        P(),
        P(),
        P(),
    )
    out_specs = P(span + mp, None)
    return jax.shard_map(local, mesh=fine, in_specs=in_specs, out_specs=out_specs, check_vma=False)
```

```python
import functools
import math

import jax
import jax.numpy as jnp
from jax import lax
from jax.experimental import pallas as pl
from jax.experimental.pallas import tpu as pltpu
from jax.sharding import Mesh, PartitionSpec as P

HD = 128
HEADS_HERE = 3
NZ, NXH, NY, NXL, NC = 8, 2, 4, 2, 2
X_FIRST = 2688
CHUNK = 16
UP = 2
LOG2E = math.log2(math.e)
SWAP = [(0, 1), (1, 0)]


def shift(value, axis, count, steps):
    return lax.ppermute(value, axis, [(i, (i + steps) % count) for i in range(count)])


def attend_body(fresh, last, flags, *refs):
    refs = list(refs)
    scalar_ref, q_ref = refs.pop(0), refs.pop(0)
    scores_ref, probs_ref = refs.pop(), refs.pop()
    if last:
        clean = (refs.pop(), refs.pop())
        peak_ref, total_ref, out_ref = refs.pop(), refs.pop(), refs.pop()
    else:
        total_ref, peak_ref = refs.pop(), refs.pop()
    if not fresh:
        old_total_ref, old_peak_ref = refs.pop(), refs.pop()
        peak_ref[...] = old_peak_ref[...]
        total_ref[...] = old_total_ref[...]
    if last:
        pieces = refs
        piece_rows = pieces[0].shape[1]

        @pl.when(pl.program_id(0) == 0)
        def _():
            for number, piece in enumerate(pieces):
                for side in range(2):
                    clean[side][pl.ds(number * piece_rows, piece_rows)] = piece[side]

        blocks = [clean]
    else:
        if len(refs) == 1:
            refs = [refs[0].at[0], refs[0].at[1]]
        blocks = list(zip(refs[::2], refs[1::2]))
    factor = HD ** (-0.5) * LOG2E
    tile = probs_ref.shape[1]
    ones = jnp.ones((blocks[0][0].shape[0], HD), jnp.bfloat16)
    y, xl, core = scalar_ref[4], scalar_ref[5], scalar_ref[6]
    places = []
    for xl_step in range(NXL):
        for y_step in range(NY):
            y_there = lax.rem(y + y_step, NY)
            xl_there = lax.rem(xl + xl_step, NXL)
            places.append((y_there * NXL + xl_there) * NC + lax.rem(core + pl.program_id(0), NC))

    def one_block(first, k_ref, v_ref):
        def take_scores(head):
            cols = slice(head * HD, (head + 1) * HD)
            rows = jnp.concatenate([q_ref[place, :, cols] for place in places], axis=0)
            scores_ref[head % 2] = lax.dot_general(
                rows, k_ref[:, cols], (((1,), (1,)), ((), ())), preferred_element_type=jnp.float32
            )

        take_scores(0)
        for head in range(HEADS_HERE):
            cols = slice(head * HD, (head + 1) * HD)
            if head + 1 < HEADS_HERE:
                take_scores(head + 1)
            scales = []
            for low in range(0, tile, CHUNK):
                rows = slice(low, low + CHUNK)
                scores = scores_ref[head % 2, rows]
                peak = jnp.max(scores, axis=1, keepdims=True)
                if not first:
                    old_peak = peak_ref[head, rows]
                    peak = jnp.maximum(old_peak, peak)
                    scales.append(jnp.exp2((old_peak - peak) * factor))
                probs_ref[head % 2, rows] = jnp.exp2(((scores - peak) * factor).astype(jnp.bfloat16))
                peak_ref[head, rows] = peak
            wide = jnp.concatenate([v_ref[:, cols], ones], axis=1)
            added = jnp.dot(probs_ref[head % 2], wide, preferred_element_type=jnp.float32)
            total_ref[head] = added if first else total_ref[head] * jnp.concatenate(scales, axis=0) + added

    for number, (k_ref, v_ref) in enumerate(blocks):
        if fresh and number == 0:
            one_block(True, k_ref, v_ref)
        else:
            pl.when(scalar_ref[flags[number]] == 1)(functools.partial(one_block, False, k_ref, v_ref))
    if last:
        for head in range(HEADS_HERE):
            total = total_ref[head]
            out_ref[:, head * HD : (head + 1) * HD] = (total[:, :HD] / total[:, HD:]).astype(jnp.bfloat16)


def attend(scalars, queries, flags, blocks, state=None, last=False):
    rows, width = queries.shape
    fresh = state is None
    share = rows // (NY * NXL * NC)
    tile = rows // NC
    count = len(flags)
    state_specs = [
        pl.BlockSpec((HEADS_HERE, tile, 1), lambda i, *_: (0, i, 0)),
        pl.BlockSpec((HEADS_HERE, tile, 2 * HD), lambda i, *_: (0, i, 0)),
    ]
    in_specs = [pl.BlockSpec((NY * NXL * NC, share, width), lambda i, *_: (0, 0, 0))]
    in_specs += [pl.BlockSpec(block.shape, lambda i, *_, rank=block.ndim: (0,) * rank) for block in blocks]
    operands = [queries.reshape(NY * NXL * NC, share, width), *blocks]
    if not fresh:
        in_specs += state_specs
        operands += state
    scratch = [pltpu.VMEM((2, tile, rows), jnp.bfloat16), pltpu.VMEM((2, tile, rows), jnp.float32)]
    if last:
        out_shape = jax.ShapeDtypeStruct((rows, width), jnp.bfloat16)
        out_specs = pl.BlockSpec((tile, width), lambda i, *_: (i, 0))
        scratch = [
            pltpu.VMEM((HEADS_HERE, tile, 2 * HD), jnp.float32),
            pltpu.VMEM((HEADS_HERE, tile, 1), jnp.float32),
            pltpu.VMEM((rows, width), jnp.bfloat16),
            pltpu.VMEM((rows, width), jnp.bfloat16),
        ] + scratch
    else:
        out_shape = [
            jax.ShapeDtypeStruct((HEADS_HERE, rows, 1), jnp.float32),
            jax.ShapeDtypeStruct((HEADS_HERE, rows, 2 * HD), jnp.float32),
        ]
        out_specs = state_specs
    return pl.pallas_call(
        functools.partial(attend_body, fresh, last, flags),
        out_shape=out_shape,
        grid_spec=pltpu.PrefetchScalarGridSpec(
            num_scalar_prefetch=1, grid=(NC,), in_specs=in_specs, out_specs=out_specs, scratch_shapes=scratch
        ),
        compiler_params=pltpu.CompilerParams(vmem_limit_bytes=40 * 1024 * 1024),
        cost_estimate=pl.CostEstimate(
            flops=4 * count * rows * rows * width, bytes_accessed=20 * rows * width, transcendentals=3 * count * rows * rows
        ),
    )(scalars, *operands)


def fetch(keys, values, root, z, xh, scalars, first_pass):
    rows, width = keys.shape
    cut = rows // NZ
    own = jnp.stack([keys.reshape(NZ, cut, width), values.reshape(NZ, cut, width)], axis=1)
    distance = lax.rem(z - root // NXH + NZ, NZ)
    at_root = distance == 0
    lag2_keys = shift(keys, "z", NZ, 1)
    down = shift(own[UP + 1], "z", NZ, -1)
    for number in range(UP + 2, NZ):
        if number == UP + 3:
            down, scalars = lax.optimization_barrier((down, scalars))
        if number == UP + 4:
            down, lag2_keys = lax.optimization_barrier((down, lag2_keys))
        down = shift(jnp.where(at_root, own[number], down), "z", NZ, -1)
    up, lag2_keys = lax.optimization_barrier((own[UP], lag2_keys))
    for number in range(UP, 0, -1):
        up = shift(jnp.where(at_root, own[number], up) if number < UP else up, "z", NZ, 1)
    values_late, up = lax.optimization_barrier((values, up))
    lag2_values = shift(values_late, "z", NZ, 1)
    piece = jnp.where(at_root, own[0], jnp.where(distance <= UP, up, down))
    piece = jnp.where(xh == lax.rem(root, NXH), piece, lax.ppermute(piece, "xh", SWAP))
    piece, lag2_values = lax.optimization_barrier((piece, lag2_values))
    lag1 = jnp.where(xh == 0, jnp.stack([keys, values]), jnp.stack([lag2_keys, lag2_values]))
    lag1 = lax.ppermute(lag1, "xh", SWAP)
    peak, total = first_pass(scalars, [lag2_keys, lag2_values])
    pieces = [piece]
    up = down = piece
    for number in range(4):
        if number == 1:
            up, peak = lax.optimization_barrier((up, peak))
        up = shift(up, "z", NZ, 1)
        pieces.append(up)
        if number < 3:
            down = shift(down, "z", NZ, -1)
            pieces.append(down)
    return [peak, total], lag1, pieces, scalars


def add(*terms):
    total = terms[0].astype(jnp.float32)
    for term in terms[1:]:
        total = total + term.astype(jnp.float32)
    return total


def sum_over_y(terms):
    half = terms[0].shape[-1] // 2
    from_below = shift(terms[2][..., :half], "y", NY, 1)
    from_above = shift(terms[2][..., half:], "y", NY, -1)
    rise = jnp.concatenate([add(terms[1][..., :half], from_below).astype(jnp.bfloat16), terms[1][..., half:]], axis=-1)
    fall = jnp.concatenate([terms[3][..., :half], add(terms[3][..., half:], from_above).astype(jnp.bfloat16)], axis=-1)
    return [terms[0], shift(rise, "y", NY, 1), shift(fall, "y", NY, -1)]


def local(queries, keys, values, residual, out_weight, gate_table, noise_steps, windows):
    z, xh, y, xl, core = (lax.axis_index(name) for name in ("z", "xh", "y", "xl", "c"))
    my_span = z * NXH + xh
    span_ids = lax.iota(jnp.int32, NZ * NXH)
    clean_root = jnp.sum(span_ids * (noise_steps == 0).astype(jnp.int32))
    rows, width = queries.shape
    share = residual.shape[0]

    weight = jnp.concatenate([out_weight, lax.ppermute(out_weight, "c", SWAP)], axis=0)
    scalars = jnp.stack(
        [
            jnp.int32(1),
            windows[my_span, 1],
            windows[my_span, 0],
            (my_span != clean_root).astype(jnp.int32),
            y,
            xl,
            core,
        ]
    )

    def first_pass(scalars, lag2):
        return attend(scalars, queries, (0, 1), [keys, values, *lag2])

    state, lag1, pieces, scalars = fetch(keys, values, clean_root, z, xh, scalars, first_pass)
    state = attend(scalars, queries, (2,), [lag1], state)
    state, weight = lax.optimization_barrier((state, weight))
    attended = attend(scalars, queries, (3,), pieces, state, last=True)
    taken = lax.ppermute(attended[rows // 2 :], "c", SWAP)
    both = jnp.concatenate([attended[: rows // 2], taken], axis=1)

    def project(low, high):
        terms = jnp.dot(both, weight[:, low:high], preferred_element_type=jnp.float32).astype(jnp.bfloat16)
        return terms.reshape(NXL, NY, share, high - low)

    x_first = project(0, X_FIRST)
    y_first = project(X_FIRST, out_weight.shape[1])

    x_got = lax.ppermute(x_first[1], "xl", SWAP)
    here = sum_over_y([y_first[:, number] for number in range(NY)])
    here_kept = [term[0] for term in here]
    here_sent = add(*[term[1] for term in here]).astype(jnp.bfloat16)
    here_got = lax.ppermute(here_sent, "xl", SWAP)
    x_sum = add(x_first[0], x_got).astype(jnp.bfloat16)
    left = add(x_sum[0], *[shift(x_sum[step], "y", NY, step) for step in (1, 3, 2)])
    right = add(*here_kept, here_got)
    gate_row = lax.dynamic_slice_in_dim(gate_table, noise_steps[my_span], 1, 0)
    summed = jnp.concatenate([left, right], axis=1)
    return (residual.astype(jnp.float32) + gate_row * summed).astype(jnp.bfloat16)


def solution(mesh):
    fine = Mesh(mesh.devices.reshape(NZ, NXH, NY, NXL, NC), ("z", "xh", "y", "xl", "c"))
    span, mp = ("z", "xh"), ("y", "xl", "c")
    in_specs = (
        P(span, mp),
        P(span, mp),
        P(span, mp),
        P(span + mp, None),
        P(mp, None),
        P(),
        P(),
        P(),
    )
    out_specs = P(span + mp, None)
    return jax.shard_map(local, mesh=fine, in_specs=in_specs, out_specs=out_specs, check_vma=False)
```

```python
import functools
import math

import jax
import jax.numpy as jnp
from jax import lax
from jax.experimental import pallas as pl
from jax.experimental.pallas import tpu as pltpu
from jax.sharding import Mesh, PartitionSpec as P

HD = 128
HEADS_HERE = 3
NZ, NXH, NY, NXL, NC = 8, 2, 4, 2, 2
X_FIRST = 2688
CHUNK = 16
UP = 2
LOG2E = math.log2(math.e)
SWAP = [(0, 1), (1, 0)]


def shift(value, axis, count, steps):
    return lax.ppermute(value, axis, [(i, (i + steps) % count) for i in range(count)])


def attend_body(fresh, last, flags, *refs):
    refs = list(refs)
    scalar_ref, q_ref = refs.pop(0), refs.pop(0)
    scores_ref, probs_ref = refs.pop(), refs.pop()
    if last:
        clean = (refs.pop(), refs.pop())
        peak_ref, total_ref, out_ref = refs.pop(), refs.pop(), refs.pop()
    else:
        total_ref, peak_ref = refs.pop(), refs.pop()
    if not fresh:
        old_total_ref, old_peak_ref = refs.pop(), refs.pop()
        peak_ref[...] = old_peak_ref[...]
        total_ref[...] = old_total_ref[...]
    if last:
        pieces = refs
        piece_rows = pieces[0].shape[1]

        @pl.when(pl.program_id(0) == 0)
        def _():
            for number, piece in enumerate(pieces):
                for side in range(2):
                    clean[side][pl.ds(number * piece_rows, piece_rows)] = piece[side]

        blocks = [clean]
    else:
        if len(refs) == 1:
            refs = [refs[0].at[0], refs[0].at[1]]
        blocks = list(zip(refs[::2], refs[1::2]))
    factor = HD ** (-0.5) * LOG2E
    tile = probs_ref.shape[1]
    ones = jnp.ones((blocks[0][0].shape[0], HD), jnp.bfloat16)
    y, xl, core = scalar_ref[4], scalar_ref[5], scalar_ref[6]
    places = []
    for xl_step in range(NXL):
        for y_step in range(NY):
            y_there = lax.rem(y + y_step, NY)
            xl_there = lax.rem(xl + xl_step, NXL)
            places.append((y_there * NXL + xl_there) * NC + lax.rem(core + pl.program_id(0), NC))

    def one_block(first, k_ref, v_ref):
        def take_scores(head):
            cols = slice(head * HD, (head + 1) * HD)
            rows = jnp.concatenate([q_ref[place, :, cols] for place in places], axis=0)
            scores_ref[head % 2] = lax.dot_general(
                rows, k_ref[:, cols], (((1,), (1,)), ((), ())), preferred_element_type=jnp.float32
            )

        take_scores(0)
        for head in range(HEADS_HERE):
            cols = slice(head * HD, (head + 1) * HD)
            if head + 1 < HEADS_HERE:
                take_scores(head + 1)
            scales = []
            for low in range(0, tile, CHUNK):
                rows = slice(low, low + CHUNK)
                scores = scores_ref[head % 2, rows]
                peak = jnp.max(scores, axis=1, keepdims=True)
                if not first:
                    old_peak = peak_ref[head, rows]
                    peak = jnp.maximum(old_peak, peak)
                    scales.append(jnp.exp2((old_peak - peak) * factor))
                probs_ref[head % 2, rows] = jnp.exp2(((scores - peak) * factor).astype(jnp.bfloat16))
                peak_ref[head, rows] = peak
            wide = jnp.concatenate([v_ref[:, cols], ones], axis=1)
            added = jnp.dot(probs_ref[head % 2], wide, preferred_element_type=jnp.float32)
            total_ref[head] = added if first else total_ref[head] * jnp.concatenate(scales, axis=0) + added

    for number, (k_ref, v_ref) in enumerate(blocks):
        if fresh and number == 0:
            one_block(True, k_ref, v_ref)
        else:
            pl.when(scalar_ref[flags[number]] == 1)(functools.partial(one_block, False, k_ref, v_ref))
    if last:
        for head in range(HEADS_HERE):
            total = total_ref[head]
            out_ref[:, head * HD : (head + 1) * HD] = (total[:, :HD] / total[:, HD:]).astype(jnp.bfloat16)


def attend(scalars, queries, flags, blocks, state=None, last=False):
    rows, width = queries.shape
    fresh = state is None
    share = rows // (NY * NXL * NC)
    tile = rows // NC
    count = len(flags)
    state_specs = [
        pl.BlockSpec((HEADS_HERE, tile, 1), lambda i, *_: (0, i, 0)),
        pl.BlockSpec((HEADS_HERE, tile, 2 * HD), lambda i, *_: (0, i, 0)),
    ]
    in_specs = [pl.BlockSpec((NY * NXL * NC, share, width), lambda i, *_: (0, 0, 0))]
    in_specs += [pl.BlockSpec(block.shape, lambda i, *_, rank=block.ndim: (0,) * rank) for block in blocks]
    operands = [queries.reshape(NY * NXL * NC, share, width), *blocks]
    if not fresh:
        in_specs += state_specs
        operands += state
    scratch = [pltpu.VMEM((2, tile, rows), jnp.bfloat16), pltpu.VMEM((2, tile, rows), jnp.float32)]
    if last:
        out_shape = jax.ShapeDtypeStruct((rows, width), jnp.bfloat16)
        out_specs = pl.BlockSpec((tile, width), lambda i, *_: (i, 0))
        scratch = [
            pltpu.VMEM((HEADS_HERE, tile, 2 * HD), jnp.float32),
            pltpu.VMEM((HEADS_HERE, tile, 1), jnp.float32),
            pltpu.VMEM((rows, width), jnp.bfloat16),
            pltpu.VMEM((rows, width), jnp.bfloat16),
        ] + scratch
    else:
        out_shape = [
            jax.ShapeDtypeStruct((HEADS_HERE, rows, 1), jnp.float32),
            jax.ShapeDtypeStruct((HEADS_HERE, rows, 2 * HD), jnp.float32),
        ]
        out_specs = state_specs
    return pl.pallas_call(
        functools.partial(attend_body, fresh, last, flags),
        out_shape=out_shape,
        grid_spec=pltpu.PrefetchScalarGridSpec(
            num_scalar_prefetch=1, grid=(NC,), in_specs=in_specs, out_specs=out_specs, scratch_shapes=scratch
        ),
        compiler_params=pltpu.CompilerParams(vmem_limit_bytes=40 * 1024 * 1024),
        cost_estimate=pl.CostEstimate(
            flops=4 * count * rows * rows * width, bytes_accessed=20 * rows * width, transcendentals=3 * count * rows * rows
        ),
    )(scalars, *operands)


def fetch(keys, values, root, z, xh, scalars, first_pass):
    rows, width = keys.shape
    cut = rows // NZ
    own = jnp.stack([keys.reshape(NZ, cut, width), values.reshape(NZ, cut, width)], axis=1)
    distance = lax.rem(z - root // NXH + NZ, NZ)
    at_root = distance == 0
    lag2_keys = shift(keys, "z", NZ, 1)
    down = shift(own[UP + 1], "z", NZ, -1)
    for number in range(UP + 2, NZ):
        if number == UP + 3:
            down, scalars = lax.optimization_barrier((down, scalars))
        if number == UP + 4:
            down, lag2_keys = lax.optimization_barrier((down, lag2_keys))
        down = shift(jnp.where(at_root, own[number], down), "z", NZ, -1)
    up, lag2_keys = lax.optimization_barrier((own[UP], lag2_keys))
    for number in range(UP, 0, -1):
        up = shift(jnp.where(at_root, own[number], up) if number < UP else up, "z", NZ, 1)
    values_late, up = lax.optimization_barrier((values, up))
    lag2_values = shift(values_late, "z", NZ, 1)
    piece = jnp.where(at_root, own[0], jnp.where(distance <= UP, up, down))
    piece = jnp.where(xh == lax.rem(root, NXH), piece, lax.ppermute(piece, "xh", SWAP))
    piece, lag2_values = lax.optimization_barrier((piece, lag2_values))
    lag1 = jnp.where(xh == 0, jnp.stack([keys, values]), jnp.stack([lag2_keys, lag2_values]))
    lag1 = lax.ppermute(lag1, "xh", SWAP)
    peak, total = first_pass(scalars, [lag2_keys, lag2_values])
    pieces = [piece]
    up = down = piece
    for number in range(4):
        if number == 1:
            up, peak = lax.optimization_barrier((up, peak))
        if number == 3:
            up, lag1 = lax.optimization_barrier((up, lag1))
        up = shift(up, "z", NZ, 1)
        pieces.append(up)
        if number < 3:
            down = shift(down, "z", NZ, -1)
            pieces.append(down)
    return [peak, total], lag1, pieces, scalars


def add(*terms):
    total = terms[0].astype(jnp.float32)
    for term in terms[1:]:
        total = total + term.astype(jnp.float32)
    return total


def sum_over_y(terms):
    half = terms[0].shape[-1] // 2
    from_below = shift(terms[2][..., :half], "y", NY, 1)
    from_above = shift(terms[2][..., half:], "y", NY, -1)
    rise = jnp.concatenate([add(terms[1][..., :half], from_below).astype(jnp.bfloat16), terms[1][..., half:]], axis=-1)
    fall = jnp.concatenate([terms[3][..., :half], add(terms[3][..., half:], from_above).astype(jnp.bfloat16)], axis=-1)
    return [terms[0], shift(rise, "y", NY, 1), shift(fall, "y", NY, -1)]


def local(queries, keys, values, residual, out_weight, gate_table, noise_steps, windows):
    z, xh, y, xl, core = (lax.axis_index(name) for name in ("z", "xh", "y", "xl", "c"))
    my_span = z * NXH + xh
    span_ids = lax.iota(jnp.int32, NZ * NXH)
    clean_root = jnp.sum(span_ids * (noise_steps == 0).astype(jnp.int32))
    rows, width = queries.shape
    share = residual.shape[0]

    weight = jnp.concatenate([out_weight, lax.ppermute(out_weight, "c", SWAP)], axis=0)
    scalars = jnp.stack(
        [
            jnp.int32(1),
            windows[my_span, 1],
            windows[my_span, 0],
            (my_span != clean_root).astype(jnp.int32),
            y,
            xl,
            core,
        ]
    )

    def first_pass(scalars, lag2):
        return attend(scalars, queries, (0, 1), [keys, values, *lag2])

    state, lag1, pieces, scalars = fetch(keys, values, clean_root, z, xh, scalars, first_pass)
    state, weight = lax.optimization_barrier((state, weight))
    state = attend(scalars, queries, (2,), [lag1], state)
    attended = attend(scalars, queries, (3,), pieces, state, last=True)
    taken = lax.ppermute(attended[rows // 2 :], "c", SWAP)
    both = jnp.concatenate([attended[: rows // 2], taken], axis=1)

    def project(low, high):
        terms = jnp.dot(both, weight[:, low:high], preferred_element_type=jnp.float32).astype(jnp.bfloat16)
        return terms.reshape(NXL, NY, share, high - low)

    x_first = project(0, X_FIRST)
    y_first = project(X_FIRST, out_weight.shape[1])

    x_got = lax.ppermute(x_first[1], "xl", SWAP)
    here = sum_over_y([y_first[:, number] for number in range(NY)])
    here_kept = [term[0] for term in here]
    here_sent = add(*[term[1] for term in here]).astype(jnp.bfloat16)
    here_got = lax.ppermute(here_sent, "xl", SWAP)
    x_sum = add(x_first[0], x_got).astype(jnp.bfloat16)
    left = add(x_sum[0], *[shift(x_sum[step], "y", NY, step) for step in (1, 3, 2)])
    right = add(*here_kept, here_got)
    gate_row = lax.dynamic_slice_in_dim(gate_table, noise_steps[my_span], 1, 0)
    summed = jnp.concatenate([left, right], axis=1)
    return (residual.astype(jnp.float32) + gate_row * summed).astype(jnp.bfloat16)


def solution(mesh):
    fine = Mesh(mesh.devices.reshape(NZ, NXH, NY, NXL, NC), ("z", "xh", "y", "xl", "c"))
    span, mp = ("z", "xh"), ("y", "xl", "c")
    in_specs = (
        P(span, mp),
        P(span, mp),
        P(span, mp),
        P(span + mp, None),
        P(mp, None),
        P(),
        P(),
        P(),
    )
    out_specs = P(span + mp, None)
    return jax.shard_map(local, mesh=fine, in_specs=in_specs, out_specs=out_specs, check_vma=False)
```
